32 devices in a mesh: seq: 16 (over z, y, core), tp: 2 (over x).
Axes of the slice: x: 2, y: 2, z: 4, core: 2. Of those that a mesh axis runs over, the one named last changes fastest.
Arguments:
- hidden_in: bfloat16 [384, 8192], P('seq', 'tp'), may hold values from -8 to 8
- kv_weight: bfloat16 [8192, 1024], P('tp'), may hold values from -0.0625 to 0.0625
- queries: bfloat16 [384, 4096], P('seq', 'tp'), may hold values from -15 to 15
- prefix_keys: bfloat16 [128, 128, 512], P('seq', None, 'tp'), may hold values from -6 to 6
- prefix_values: bfloat16 [128, 128, 512], P('seq', None, 'tp'), may hold values from -6 to 6
- page_table: int32 [128], replicated, may hold values from 0 to 127, each once
- suffix_lengths: int32 [2, 8], replicated, may hold values from 1 to 160, 192 in all within a row
- out_weight: bfloat16 [4096, 4096], P('tp'), may hold values from -0.09375 to 0.09375
Outputs:
- hidden: bfloat16 [384, 4096], P('seq', 'tp')
- new_pages: bfloat16 [384, 1024], P('seq', 'tp')
The draws below stay inside these ranges and needn't reach their ends.
Inputs may be any that keep to these rules, and one draw needn't show every extreme that they name: `page_table`: a permutation of the 128 cache pages; entries 64 * g to 64 * g + 63 are group g's prefix pages. `suffix_lengths`: each row sums to 192; group g's requests take its suffix tokens in order of their place u; some request has exactly 160 tokens.
All inputs are finite; a program needn't handle non-finite values.
Results may differ from the reference program's by a relative error of at most 0.0095.
Values may be sent and summed in bfloat16 or wider, within the bound.
No kernel may reach another device: no remote copies, remote signals or barrier semaphores. Data moves between devices by JAX's collectives and lax.ppermute only.
A program may use at most 192 MiB of HBM per device.

```python
import math
import jax
import jax.numpy as jnp
import numpy as np
from jax import lax

D = 8192
DOUT = 4096
QH = 32
KVH = 4
HD = 128
PAGE = 128
GROUPS = 2
REQS = 8
S_DEV = 24
SUFFIX = 384
HALF = 192
POOL = 128
GROUP_PAGES = 64
PREFIX = 8192
LMAX = 160


def draw_queries(key, part):
    noise_key = jax.random.fold_in(key, 11)
    full_shape = (SUFFIX, QH * HD)
    return (2.5 * jax.random.truncated_normal(noise_key, -6.0, 6.0, full_shape)).astype(jnp.bfloat16)


def draw_prefix_keys(key, part):
    noise_key = jax.random.fold_in(key, 23)
    full_shape = (POOL, PAGE, KVH * HD)
    return jax.random.truncated_normal(noise_key, -6.0, 6.0, full_shape).astype(jnp.bfloat16)


def block_scale(stream_key, dims, pieces, smallest, largest):
    level = 1.0
    for dim, shards_of in pieces:
        heights = jax.random.uniform(jax.random.fold_in(jax.random.fold_in(stream_key, 6), dim), (shards_of,), jnp.float32, smallest / len(pieces), largest / len(pieces))
        level = level * jnp.repeat(jnp.exp(heights), dims[dim] // shards_of).reshape((-1,) + (1,) * (len(dims) - 1 - dim))
    return level


def split_up(number_of, total, most, slope):
    weights = [(1 << 20) // math.isqrt(standing ** slope) + 1 for standing in range(2, number_of + 1)]
    rest, holding = total - most - (number_of - 1), [1] * (number_of - 1)
    while rest > 0:
        movable = [i for i in range(number_of - 1) if holding[i] < most]
        pool, left = sum([weights[i] for i in movable]), rest
        for i in movable:
            extra = min(most - holding[i], max(1, left * weights[i] // pool), rest)
            holding[i] = holding[i] + extra
            rest = rest - extra
    return np.array([most] + holding)


def ragged_sizes(stream_key, count, total, bound, skew):
    if count == 2:
        one = jax.random.randint(stream_key, (), max(1, total - bound), min(bound, total - 1) + 1)
        return jnp.stack([one, total - one])
    sizes = jnp.asarray(split_up(count, total, bound, skew), jnp.int32)
    twos = (count - 1) // 2
    donor, taker = sizes[1:1 + 2 * twos:2], sizes[2:2 + 2 * twos:2]
    slack = jnp.minimum(donor - 1, bound - taker)
    moved = jax.random.randint(jax.random.fold_in(stream_key, 1), (twos,), 0, 1 << 20) % (slack + 1)
    sizes = sizes.at[1:1 + 2 * twos:2].set(donor - moved).at[2:2 + 2 * twos:2].set(taker + moved)
    return sizes[jax.random.permutation(jax.random.fold_in(stream_key, 2), count)]


def gaussian(stream_key, extent, scale, most, cuts=(), kind=jnp.bfloat16):
    drawn = scale * jax.random.normal(stream_key, extent, jnp.float32)
    if cuts:
        drawn = drawn * block_scale(stream_key, extent, cuts, -0.22, 0.18)
    return jnp.clip(drawn, -most, most).astype(kind)


def setup_inputs(seed: int = 0) -> dict:
    streams_of = jax.random.split(jax.random.key(seed), 9)
    hidden_in = gaussian(streams_of[0], (SUFFIX, D), 1.6, 8.0, ((0, 16), (1, 2)))
    kv_weight = gaussian(streams_of[1], (D, KVH * 2 * HD), D ** -0.5, 0.0625, ((0, 2),))
    queries = draw_queries(jax.random.fold_in(streams_of[8], 71), 0)
    prefix_keys = draw_prefix_keys(jax.random.fold_in(streams_of[8], 71), 0)
    prefix_values = gaussian(streams_of[4], (POOL, PAGE, KVH * HD), 1.0, 6.0, ((0, 16), (2, 2)))
    page_table = jax.random.permutation(streams_of[5], POOL).astype(jnp.int32)
    suffix_lengths = jax.vmap(lambda own: ragged_sizes(own, REQS, HALF, LMAX, 2))(jax.random.split(streams_of[6], GROUPS)).reshape((GROUPS, REQS)).astype(jnp.int32)
    out_weight = gaussian(streams_of[7], (QH * HD, DOUT), (QH * HD) ** -0.5, 0.09375, ((0, 2),))
    return dict(hidden_in=hidden_in, kv_weight=kv_weight, queries=queries, prefix_keys=prefix_keys, prefix_values=prefix_values, page_table=page_table, suffix_lengths=suffix_lengths, out_weight=out_weight)


masked_score = -1e+30

def place_tokens(tokens, block_rows):
    blocks = tokens // block_rows
    groups = (blocks % GROUPS).astype(jnp.int32)
    within = (blocks // GROUPS * block_rows + tokens % block_rows).astype(jnp.int32)
    return (groups, within)

def token_table(groups, within, lengths):
    picker = (groups[:, None] == jnp.arange(GROUPS, dtype=jnp.int32)[None, :]).astype(jnp.int32)
    end_marks = jnp.cumsum(lengths, axis=1).astype(jnp.int32)
    token_ends = lax.optimization_barrier(jnp.sum(picker[:, :, None] * end_marks[None, :, :], axis=1))
    token_lens = lax.optimization_barrier(jnp.sum(picker[:, :, None] * lengths[None, :, :], axis=1))
    passed = (within[:, None] >= token_ends).astype(jnp.int32)
    request = lax.optimization_barrier(jnp.sum(passed, axis=1)).astype(jnp.int32)
    offset = (within - lax.optimization_barrier(jnp.sum(passed * token_lens, axis=1))).astype(jnp.int32)
    return (groups * REQS + request, offset)

def rotate(key_rows, positions):
    half_dim = HD // 2
    frequency = jnp.power(500000.0, -(jnp.arange(half_dim, dtype=jnp.float32) * 2.0 / HD))
    angles = positions.astype(jnp.float32)[:, None] * frequency[None, :]
    cosine = jnp.cos(angles)[:, None, :]
    sine_part = jnp.sin(angles)[:, None, :]
    leading = key_rows[..., :half_dim]
    trailing = key_rows[..., half_dim:]
    return jnp.concatenate([leading * cosine - trailing * sine_part, trailing * cosine + leading * sine_part], axis=-1)

def rounded(weights):
    narrow = lax.optimization_barrier(weights.astype(jnp.bfloat16))
    return narrow.astype(jnp.float32)

def reference(hidden_in, kv_weight, queries, prefix_keys, prefix_values, page_table, suffix_lengths, out_weight):
    tokens = jnp.arange(SUFFIX, dtype=jnp.int32)
    groups, within = place_tokens(tokens, S_DEV)
    request_ids, offsets = token_table(groups, within, suffix_lengths)
    projected = jnp.dot(hidden_in, kv_weight, preferred_element_type=jnp.float32).reshape(SUFFIX, KVH, 2, HD)
    rotated = rotate(projected[:, :, 0], PREFIX + offsets)
    new_pages = jnp.stack([rotated, projected[:, :, 1]], axis=2).reshape(SUFFIX, KVH * 2 * HD).astype(jnp.bfloat16)
    page_kv = new_pages.reshape(SUFFIX, KVH, 2, HD).astype(jnp.float32)
    page_rows = page_table.reshape(GROUPS, GROUP_PAGES)
    score_scale = 1.0 / math.sqrt(HD)
    group_q = QH // KVH
    highest = lax.Precision.HIGHEST
    places = jnp.arange(HALF, dtype=jnp.int32)

    def one_block(block_index):
        first_row = (block_index * S_DEV).astype(jnp.int32)
        group_index = (block_index % GROUPS).astype(jnp.int32)
        first_place = (block_index // GROUPS * S_DEV).astype(jnp.int32)
        query_block = lax.dynamic_slice_in_dim(queries, first_row, S_DEV, 0).astype(jnp.float32)
        query_block = query_block.reshape(S_DEV, KVH, group_q, HD)
        slot_ids = lax.dynamic_index_in_dim(page_rows, group_index, 0, keepdims=False)
        cache_keys = jnp.take(prefix_keys, slot_ids, axis=0).astype(jnp.float32).reshape(PREFIX, KVH, HD)
        cache_vals = jnp.take(prefix_values, slot_ids, axis=0).astype(jnp.float32).reshape(PREFIX, KVH, HD)
        prefix_scores = jnp.einsum('tkgd,pkd->tkgp', query_block, cache_keys, precision=highest) * score_scale
        group_tokens = (places // S_DEV * GROUPS + group_index) * S_DEV + places % S_DEV
        own_kv = jnp.take(page_kv, group_tokens, axis=0)
        own_ids = jnp.take(request_ids, group_tokens, axis=0)
        row_ids = lax.dynamic_slice_in_dim(request_ids, first_row, S_DEV, 0)
        row_pos = first_place + jnp.arange(S_DEV, dtype=jnp.int32)
        visible = (own_ids[None, :] == row_ids[:, None]) & (places[None, :] <= row_pos[:, None])
        suffix_scores = jnp.einsum('tkgd,pkd->tkgp', query_block, own_kv[:, :, 0], precision=highest) * score_scale
        suffix_scores = jnp.where(visible[:, None, None, :], suffix_scores, masked_score)
        row_top = jnp.maximum(lax.optimization_barrier(jnp.max(prefix_scores, axis=-1)), lax.optimization_barrier(jnp.max(suffix_scores, axis=-1)))
        prefix_weight = jnp.exp(prefix_scores - row_top[..., None])
        suffix_weight = jnp.exp(suffix_scores - row_top[..., None]) * visible[:, None, None, :].astype(jnp.float32)
        row_total = lax.optimization_barrier(jnp.sum(prefix_weight, axis=-1)) + lax.optimization_barrier(jnp.sum(suffix_weight, axis=-1))
        row_mix = jnp.einsum('tkgp,pkd->tkgd', rounded(prefix_weight), cache_vals, precision=highest)
        row_mix = row_mix + jnp.einsum('tkgp,pkd->tkgd', rounded(suffix_weight), own_kv[:, :, 1], precision=highest)
        return (row_mix / row_total[..., None]).reshape(S_DEV, QH * HD)
    attended = lax.map(one_block, jnp.arange(SUFFIX // S_DEV, dtype=jnp.int32))
    attended = attended.reshape(SUFFIX, QH * HD).astype(jnp.bfloat16)
    hidden = jnp.dot(attended, out_weight, preferred_element_type=jnp.float32).astype(jnp.bfloat16)
    return (hidden, new_pages)
```

```python
import functools
import math

import jax
import jax.numpy as jnp
from jax import lax
from jax.experimental import pallas as pl
from jax.experimental.pallas import tpu as pltpu
from jax.sharding import PartitionSpec as P

HD = 128
PAGE = 128
GROUPS = 2
REQS = 8
CHUNK = 4
LOW = -1e30
EXP2_SCALE = math.log2(math.e) / math.sqrt(HD)
F32 = jnp.float32
BF16 = jnp.bfloat16
MIB = 1 << 20

VMEM = pl.BlockSpec(memory_space=pltpu.VMEM)
SMEM = pl.BlockSpec(memory_space=pltpu.SMEM)
ANY = pl.BlockSpec(memory_space=pl.ANY)


def params(mib):
    return pltpu.CompilerParams(vmem_limit_bytes=mib * MIB)


def pack_pages(keys, values, place, splits):
    pages = keys.shape[0]

    def body(place_ref, *refs):
        half = len(refs) // 2
        for source, target in zip(refs[:half], refs[half:]):
            target[...] = source[...]

    def column(step):
        return pl.BlockSpec((pages, PAGE, HD), lambda i, place: (0, 0, place[1] ^ step))

    out = pl.BlockSpec((pages, PAGE, HD), lambda i, place: (0, 0, 0))
    shape = jax.ShapeDtypeStruct((pages, PAGE, HD), BF16)
    specs = [column(step) for step in range(splits) for _ in range(2)]
    return pl.pallas_call(
        body,
        grid_spec=pltpu.PrefetchScalarGridSpec(
            num_scalar_prefetch=1, grid=(1,), in_specs=specs, out_specs=[out] * (2 * splits)
        ),
        out_shape=[shape] * (2 * splits),
        compiler_params=params(16),
        cost_estimate=pl.CostEstimate(
            flops=0, bytes_accessed=4 * splits * pages * PAGE * HD * 2, transcendentals=0
        ),
    )(place, *([keys, values] * splits))


def finish_kv(mine, others, cosine, sine, heads):
    rows = mine.shape[0]

    def body(*refs):
        out = refs[-1]
        total = refs[0][...]
        for other in refs[1:-3]:
            total = total + other[...]
        cos, sin = refs[-3][...], refs[-2][...]
        for head in range(heads):
            key = total[:, head * 2 * HD : (head * 2 + 1) * HD]
            turned = key * cos + pltpu.roll(key, HD // 2, 1) * sin
            out[:, head * 2 * HD : (head * 2 + 1) * HD] = turned.astype(BF16)
            value = total[:, (head * 2 + 1) * HD : (head * 2 + 2) * HD]
            out[:, (head * 2 + 1) * HD : (head * 2 + 2) * HD] = value.astype(BF16)

    return pl.pallas_call(
        body,
        in_specs=[VMEM] * (3 + len(others)),
        out_specs=VMEM,
        out_shape=jax.ShapeDtypeStruct((rows, heads * 2 * HD), BF16),
    )(mine, *others, cosine, sine)


def collect_pages(page_table, place, sources, pages, splits):
    slots = pages * splits * GROUPS
    group_pages = page_table.shape[0] // GROUPS

    def body(table, place_ref, *refs):
        count = len(refs) - 7
        key_refs, value_refs = refs[0:count:2], refs[1:count:2]
        keys_out, values_out, number_out, keys, values, key_sem, value_sem = refs[count:]
        group, split = place_ref[0], place_ref[1]
        first = place_ref[2]

        def copies(which, page, at):
            rows = pl.ds(pl.multiple_of(at * PAGE, PAGE), PAGE)
            return (
                pltpu.make_async_copy(key_refs[which].at[page], keys.at[rows], key_sem.at[at]),
                pltpu.make_async_copy(
                    value_refs[which].at[page], values.at[rows, pl.ds(0, HD)], value_sem.at[at]
                ),
            )

        def look(i, number):
            slot = table[group * group_pages + i] - first
            here = jnp.logical_and(slot >= 0, slot < slots)

            @pl.when(here)
            def _():
                device = slot // pages
                page = slot - device * pages
                kind = jnp.bitwise_xor(device, split * GROUPS + group)
                for which in range(splits * GROUPS):

                    @pl.when(kind == which)
                    def _():
                        for copy in copies(which, page, number):
                            copy.start()

            return number + here.astype(jnp.int32)

        number = lax.fori_loop(0, group_pages, look, jnp.int32(0))
        number_out[0] = number
        values[:, HD:] = jnp.ones((slots * PAGE, HD), BF16)

        def clear(i, carry):
            rows = pl.ds(pl.multiple_of(i * PAGE, PAGE), PAGE)
            keys[rows, :] = jnp.zeros((PAGE, HD), BF16)
            values[rows, 0:HD] = jnp.zeros((PAGE, HD), BF16)
            return carry

        lax.fori_loop(number, slots, clear, 0)

        def land(i, carry):
            for copy in copies(0, 0, i):
                copy.wait()
            return carry

        lax.fori_loop(0, number, land, 0)
        keys_out[...] = keys[...]
        values_out[...] = values[...]

    return pl.pallas_call(
        body,
        in_specs=[SMEM, SMEM] + [ANY] * len(sources),
        out_specs=[VMEM, VMEM, SMEM],
        out_shape=[
            jax.ShapeDtypeStruct((slots * PAGE, HD), BF16),
            jax.ShapeDtypeStruct((slots * PAGE, 2 * HD), BF16),
            jax.ShapeDtypeStruct((1,), jnp.int32),
        ],
        scratch_shapes=[
            pltpu.VMEM((slots * PAGE, HD), BF16),
            pltpu.VMEM((slots * PAGE, 2 * HD), BF16),
            pltpu.SemaphoreType.DMA((slots,)),
            pltpu.SemaphoreType.DMA((slots,)),
        ],
        compiler_params=params(24),
    )(page_table, place, *sources)


def attend(number, lengths, place, far, query, suffix, keys, values, rows_each, splits):
    tokens = query.shape[0]
    heads = query.shape[1] // HD
    rows = tokens * heads
    slots = keys.shape[0] // PAGE
    chunks = -(-slots // CHUNK)
    wide = CHUNK * PAGE
    parts = -(-rows // HD)
    stat_rows = -(-3 * parts // 16) * 16

    def body(
        number_ref, len_ref, place_ref, query_ref, suffix_ref, keys_hbm, values_hbm, out,
        key_buf, value_buf, scores, top, total, column, stats, key_sem, value_sem,
    ):
        count = number_ref[0]
        turns = lax.div(count + (CHUNK - 1), CHUNK)

        def key_copy(c):
            span = pl.ds(pl.multiple_of(c * wide, wide), wide)
            return pltpu.make_async_copy(keys_hbm.at[span], key_buf.at[c], key_sem.at[c])

        def value_copy(c):
            span = pl.ds(pl.multiple_of(c * wide, wide), wide)
            return pltpu.make_async_copy(values_hbm.at[span], value_buf.at[c], value_sem.at[c])

        def begin(c, carry):
            key_copy(c).start()
            value_copy(c).start()
            return carry

        lax.fori_loop(0, turns, begin, 0)
        q = jnp.concatenate(
            [query_ref[:, h * HD : (h + 1) * HD].astype(F32) for h in range(heads)], axis=0
        ).astype(BF16)

        group, split = place_ref[0], place_ref[1]
        z_here = place_ref[3]
        z_query = jnp.bitwise_xor(z_here, far)

        def places(z, axis):
            index = lax.broadcasted_iota(jnp.int32, (tokens, tokens), axis)
            result = jnp.zeros((tokens, tokens), jnp.int32)
            for sub in range(splits):
                block = z * splits + jnp.bitwise_xor(split, sub)
                result = jnp.where(
                    index >= sub * rows_each, (block - sub) * rows_each + index, result
                )
            return result

        query_place, key_place = places(z_query, 0), places(z_here, 1)
        begins = jnp.zeros((tokens, tokens), jnp.int32)
        edge = jnp.int32(0)
        for r in range(REQS):
            edge = edge + len_ref[group, r]
            begins = jnp.where(query_place >= edge, edge, begins)
        seen = jnp.logical_and(key_place <= query_place, key_place >= begins)
        seen = jnp.concatenate([seen.astype(F32)] * heads, axis=0)
        own = lax.dot_general(
            q, suffix_ref[:, :HD], (((1,), (1,)), ((), ())), preferred_element_type=F32
        )
        own = jnp.where(seen > 0.0, own, LOW)
        top[...] = jnp.full((rows, HD), LOW, F32)

        def first_pass(c, carry):
            key_copy(c).wait()
            got = lax.dot_general(
                q, key_buf[c], (((1,), (1,)), ((), ())), preferred_element_type=F32
            )
            best = top[...]
            for j in range(CHUNK):
                piece = got[:, j * PAGE : (j + 1) * PAGE]
                piece = jnp.where(c * CHUNK + j < count, piece, LOW)
                scores[c, :, j * PAGE : (j + 1) * PAGE] = piece
                best = jnp.maximum(best, piece)
            top[...] = best
            return carry

        lax.fori_loop(0, turns, first_pass, 0)
        highest = jnp.maximum(
            jnp.max(top[...], axis=1, keepdims=True), jnp.max(own, axis=1, keepdims=True)
        )
        weights = jnp.exp2((own - highest) * EXP2_SCALE) * seen
        own_values = jnp.concatenate(
            [suffix_ref[:, HD : 2 * HD], jnp.ones((tokens, HD), BF16)], axis=1
        )
        total[...] = jnp.dot(weights.astype(BF16), own_values, preferred_element_type=F32)

        def second_pass(c, carry):
            value_copy(c).wait()
            weights = jnp.exp2((scores[c] - highest) * EXP2_SCALE).astype(BF16)
            total[...] += jnp.dot(weights, value_buf[c], preferred_element_type=F32)
            return carry

        lax.fori_loop(0, turns, second_pass, 0)
        sums = total[:, HD:]
        some = sums > 0.0
        safe = jnp.where(some, sums, 1.0)
        out[0:rows, :] = (total[:, :HD] / safe).astype(BF16)
        column[0:rows, :] = jnp.where(some, highest * EXP2_SCALE + jnp.log2(safe), LOW)
        stats[...] = jnp.zeros((stat_rows, HD), F32)
        for part in range(parts):
            line = column[part * HD : (part + 1) * HD, :].T[0:1, :]
            for piece in range(3):
                rounded = line.astype(BF16).astype(F32)
                stats[3 * part + piece : 3 * part + piece + 1, :] = rounded
                line = line - rounded
        out[rows : rows + stat_rows, :] = stats[...].astype(BF16)

    return pl.pallas_call(
        body,
        in_specs=[SMEM, SMEM, SMEM, VMEM, VMEM, ANY, ANY],
        out_specs=VMEM,
        out_shape=jax.ShapeDtypeStruct((rows + stat_rows, HD), BF16),
        scratch_shapes=[
            pltpu.VMEM((chunks, wide, HD), BF16),
            pltpu.VMEM((chunks, wide, 2 * HD), BF16),
            pltpu.VMEM((chunks, rows, wide), F32),
            pltpu.VMEM((rows, HD), F32),
            pltpu.VMEM((rows, 2 * HD), F32),
            pltpu.VMEM((parts * HD, HD), F32),
            pltpu.VMEM((stat_rows, HD), F32),
            pltpu.SemaphoreType.DMA((chunks,)),
            pltpu.SemaphoreType.DMA((chunks,)),
        ],
        compiler_params=params(32),
        cost_estimate=pl.CostEstimate(
            flops=2 * rows * slots * PAGE * HD,
            bytes_accessed=slots * PAGE * HD * 3,
            transcendentals=rows * slots * PAGE // 2,
        ),
    )(number, lengths, place, query, suffix, keys, values)


def project(place, partials, out_weight, rows_each, splits, ranks, heads):
    tokens = rows_each * splits
    rows = tokens * heads
    parts = -(-rows // HD)
    depth = heads * HD
    width = out_weight.shape[1] // ranks
    tile = min(width, 512)
    tiles = width // tile

    def body(place_ref, *refs):
        count = len(partials)
        partial_refs, weight_ref = refs[:count], refs[count]
        outs = refs[count + 1 : count + 1 + ranks * splits]
        merged, attended = refs[count + 1 + ranks * splits :]
        step = pl.program_id(0)

        @pl.when(step == 0)
        def _():
            for part in range(parts):
                length = min(HD, rows - part * HD)
                lines = []
                for ref in partial_refs:
                    stat = ref[rows:, :].astype(F32)
                    lines.append(
                        stat[3 * part : 3 * part + 1]
                        + stat[3 * part + 1 : 3 * part + 2]
                        + stat[3 * part + 2 : 3 * part + 3]
                    )
                best = functools.reduce(jnp.maximum, lines)
                shares = [jnp.exp2(line - best) for line in lines]
                whole = functools.reduce(jnp.add, shares)
                mixed = jnp.zeros((length, HD), F32)
                for share, ref in zip(shares, partial_refs):
                    factor = jnp.broadcast_to(share / whole, (HD, HD)).T[:length]
                    mixed = mixed + factor * ref[part * HD : part * HD + length, :].astype(F32)
                merged[part * HD : part * HD + length, :] = mixed
            for h in range(heads):
                attended[:, h * HD : (h + 1) * HD] = merged[
                    h * tokens : (h + 1) * tokens, :
                ].astype(BF16)

        product = jnp.dot(attended[...], weight_ref[...], preferred_element_type=F32)
        for rank in range(ranks):

            @pl.when(step // tiles == ranks - 1 - rank)
            def _():
                for sub in range(splits):
                    out = outs[rank * splits + sub]
                    piece = product[sub * rows_each : (sub + 1) * rows_each]
                    out[...] = piece.astype(out.dtype)

    def weight_at(i, place):
        rank = jnp.bitwise_xor(ranks - 1 - i // tiles, place[4])
        return (place[1], rank * tiles + i % tiles)

    def out_at(rank):
        def index(i, place):
            return (0, jnp.clip(i - (ranks - 1 - rank) * tiles, 0, tiles - 1))

        return index

    outs = [(rank, sub) for rank in range(ranks) for sub in range(splits)]
    whole_partial = pl.BlockSpec(partials[0].shape, lambda i, place: (0, 0))
    return pl.pallas_call(
        body,
        grid_spec=pltpu.PrefetchScalarGridSpec(
            num_scalar_prefetch=1,
            grid=(ranks * tiles,),
            in_specs=[whole_partial] * len(partials) + [pl.BlockSpec((depth, tile), weight_at)],
            out_specs=[pl.BlockSpec((rows_each, tile), out_at(rank)) for rank, _ in outs],
            scratch_shapes=[pltpu.VMEM((rows, HD), F32), pltpu.VMEM((tokens, depth), BF16)],
        ),
        out_shape=[
            jax.ShapeDtypeStruct((rows_each, width), F32 if pair == (0, 0) else BF16)
            for pair in outs
        ],
        compiler_params=params(32),
        cost_estimate=pl.CostEstimate(
            flops=2 * tokens * depth * width * ranks,
            bytes_accessed=depth * width * ranks * 2,
            transcendentals=0,
        ),
    )(place, *partials, out_weight)


def local(
    hidden_in,
    kv_weight,
    queries,
    prefix_keys,
    prefix_values,
    page_table,
    suffix_lengths,
    out_weight,
):
    rows = hidden_in.shape[0]
    seq_count, ranks = lax.axis_size("seq"), lax.axis_size("tp")
    seq_rank, tp_rank = lax.axis_index("seq"), lax.axis_index("tp")
    pages = prefix_keys.shape[0]
    splits = prefix_keys.shape[2] // HD
    heads = queries.shape[1] // HD // splits
    prefix_len = pages * seq_count // GROUPS * PAGE
    blocks = seq_count // GROUPS
    depth = blocks // splits
    group = seq_rank % GROUPS
    block = seq_rank // GROUPS
    split = block % splits
    place = jnp.stack(
        [group, split, (block - split) * GROUPS * pages, block // splits, tp_rank]
    ).astype(jnp.int32)

    def across(array, far=0, side=0, core=0):
        step = (far * splits + side) * GROUPS + core
        return lax.ppermute(array, "seq", [(i, i ^ step) for i in range(seq_count)])

    def columns(array, index, width):
        return lax.dynamic_slice_in_dim(array, index * width, width, 1)

    parts = [columns(queries, split, heads * HD)]
    for side in range(1, splits):
        parts.append(across(columns(queries, split ^ side, heads * HD), side=side))
    my_query = jnp.concatenate(parts, axis=0)

    packed = pack_pages(prefix_keys, prefix_values, place, splits)
    sources = []
    for side in range(splits):
        keys, values = packed[2 * side], packed[2 * side + 1]
        if side:
            keys, values = across(keys, side=side), across(values, side=side)
        sources += [keys, values, across(keys, core=1), across(values, core=1)]
    far_queries = [my_query] + [across(my_query, far=far) for far in range(1, depth)]

    partial = jnp.dot(hidden_in, kv_weight, preferred_element_type=F32)
    width = splits * 2 * HD
    others = []
    for rank in range(1, ranks):
        piece = columns(partial, tp_rank ^ rank, width)
        others.append(lax.ppermute(piece, "tp", [(i, i ^ rank) for i in range(ranks)]))
    within = block * rows + jnp.arange(rows, dtype=jnp.int32)
    lengths = jnp.sum(
        jnp.where(jnp.arange(GROUPS)[:, None] == group, suffix_lengths, 0), axis=0
    )
    ends = jnp.sum(
        jnp.where(jnp.arange(REQS)[None, :] <= jnp.arange(REQS)[:, None], lengths[None, :], 0),
        axis=1,
    )
    begins = jnp.max(jnp.where(within[:, None] >= ends[None, :], ends[None, :], 0), axis=1)
    positions = prefix_len + within - begins
    half = HD // 2
    frequency = jnp.power(500000.0, -(jnp.arange(half, dtype=F32) * 2.0 / HD))
    angles = positions.astype(F32)[:, None] * frequency[None, :]
    cosine, sine = jnp.cos(angles), jnp.sin(angles)
    cosine = jnp.concatenate([cosine, cosine], axis=1)
    sine = jnp.concatenate([-sine, sine], axis=1)
    new_pages = finish_kv(columns(partial, tp_rank, width), others, cosine, sine, splits)
    suffix = [columns(new_pages, split, 2 * HD)]
    for side in range(1, splits):
        suffix.append(across(columns(new_pages, split ^ side, 2 * HD), side=side))
    suffix = jnp.concatenate(suffix, axis=0)

    keys, values, number = collect_pages(page_table, place, sources, pages, splits)
    returned = []
    for far in range(depth - 1, -1, -1):
        partial_sum = attend(
            number, suffix_lengths, place, far, far_queries[far], suffix, keys, values, rows, splits
        )
        returned.append(across(partial_sum, far=far) if far else partial_sum)

    products = project(place, returned, out_weight, rows, splits, ranks, heads)
    hidden = products[0]
    for rank in range(ranks - 1, -1, -1):
        for side in range(splits - 1, -1, -1):
            if rank or side:
                step = side * GROUPS
                route = [
                    (i * ranks + j, (i ^ step) * ranks + (j ^ rank))
                    for i in range(seq_count)
                    for j in range(ranks)
                ]
                got = lax.ppermute(products[rank * splits + side], ("seq", "tp"), route)
                hidden = hidden + got.astype(F32)
    return (hidden.astype(BF16), new_pages)


def solution(mesh):
    return jax.shard_map(
        local,
        mesh=mesh,
        in_specs=(
            P("seq", "tp"),
            P("tp", None),
            P("seq", "tp"),
            P("seq", None, "tp"),
            P("seq", None, "tp"),
            P(),
            P(),
            P("tp", None),
        ),
        out_specs=(P("seq", "tp"), P("seq", "tp")),
        check_vma=False,
    )
```

```python
import functools
import math

import jax
import jax.numpy as jnp
from jax import lax
from jax.experimental import pallas as pl
from jax.experimental.pallas import tpu as pltpu
from jax.sharding import PartitionSpec as P

HD = 128
PAGE = 128
GROUPS = 2
REQS = 8
PLACE = 5
CHUNK = 4
BLOCKS = 2
AHEAD = 8
LOW = -1e30
EXP2_SCALE = math.log2(math.e) / math.sqrt(HD)
F32 = jnp.float32
BF16 = jnp.bfloat16
MIB = 1 << 20

NT = (((1,), (1,)), ((), ()))

VMEM = pl.BlockSpec(memory_space=pltpu.VMEM)
SMEM = pl.BlockSpec(memory_space=pltpu.SMEM)
ANY = pl.BlockSpec(memory_space=pl.ANY)
HBM = pl.BlockSpec(memory_space=pltpu.HBM)


TINY = pl.CostEstimate(flops=1, bytes_accessed=1, transcendentals=0)


def params(mib):
    return pltpu.CompilerParams(vmem_limit_bytes=mib * MIB)


def array_after(array, *awaited):
    def body(*refs):
        pass

    return pl.pallas_call(
        body,
        in_specs=[ANY] * (1 + len(awaited)),
        out_specs=ANY,
        out_shape=jax.ShapeDtypeStruct(array.shape, array.dtype),
        input_output_aliases={0: 0},
        compiler_params=params(2),
        cost_estimate=TINY,
    )(array, *awaited)


def list_pages(page_table, place, pages, splits, awaited):
    slots = pages * splits * GROUPS
    group_pages = page_table.shape[0] // GROUPS

    def body(table, place_ref, awaited_ref, out):
        for i in range(PLACE):
            out[i] = place_ref[i]
        group, first = place_ref[0], place_ref[2]

        def look(i, number):
            slot = table[group * group_pages + i] - first
            here = jnp.logical_and(slot >= 0, slot < slots)
            out[number + PLACE + 1] = slot
            return number + here.astype(jnp.int32)

        out[PLACE] = lax.fori_loop(0, group_pages, look, jnp.int32(0), unroll=8)

    return pl.pallas_call(
        body,
        in_specs=[SMEM, SMEM, ANY],
        out_specs=SMEM,
        out_shape=jax.ShapeDtypeStruct((PLACE + 2 + slots,), jnp.int32),
        compiler_params=params(2),
        cost_estimate=TINY,
    )(page_table, place, awaited)


def project_kv(hidden_in, weight, place, ranks, splits):
    rows, deep = hidden_in.shape
    width = weight.shape[1] // ranks
    steps = 8
    part = deep // steps
    kinds = [(rank, step) for rank in range(ranks) for step in range(splits)]

    def body(place_ref, hidden_ref, weight_ref, *refs):
        outs, (buffer, sums, sem) = refs[: len(kinds)], refs[len(kinds) :]
        copies = [
            pltpu.make_async_copy(weight_ref.at[pl.ds(i * part, part)], buffer.at[i], sem.at[i])
            for i in range(steps)
        ]
        for copy in copies[:AHEAD]:
            copy.start()
        for i, copy in enumerate(copies):
            copy.wait()
            if i + AHEAD < steps:
                copies[i + AHEAD].start()
            product = jnp.dot(
                hidden_ref[:, i * part : (i + 1) * part],
                buffer[i],
                preferred_element_type=F32,
            )
            sums[...] = product if i == 0 else sums[...] + product
        for out, (rank, step) in zip(outs, kinds):
            start = jnp.bitwise_xor(place_ref[4], rank) * width
            if step:
                start = start + jnp.bitwise_xor(place_ref[1], step) * (2 * HD)
            out[...] = sums[:, pl.ds(pl.multiple_of(start, 2 * HD), out.shape[1])]

    return pl.pallas_call(
        body,
        in_specs=[SMEM, VMEM, HBM],
        out_specs=[VMEM] * len(kinds),
        out_shape=[
            jax.ShapeDtypeStruct((rows, 2 * HD if step else width), F32) for _, step in kinds
        ],
        scratch_shapes=[
            pltpu.VMEM((steps, part, weight.shape[1]), BF16),
            pltpu.VMEM((rows, weight.shape[1]), F32),
            pltpu.SemaphoreType.DMA((steps,)),
        ],
        compiler_params=params(48),
        cost_estimate=TINY,
    )(place, hidden_in, weight)


def finish_kv(place, own, others, cosine, sine, heads, awaited):
    rows = own[0].shape[0]
    ranks = len(own)
    splits = 1 + len(others)

    def body(place_ref, *refs):
        own_refs, refs = refs[:ranks], refs[ranks:]
        other_refs, refs = refs[: (splits - 1) * ranks], refs[(splits - 1) * ranks :]
        cos_ref, sin_ref, _, out, suffix = refs

        def turned(key, sub):
            cos, sin = cos_ref[sub * rows : (sub + 1) * rows], sin_ref[sub * rows : (sub + 1) * rows]
            return (key * cos + pltpu.roll(key, HD // 2, 1) * sin).astype(BF16)

        total = functools.reduce(jnp.add, [ref[...] for ref in own_refs])
        pieces = []
        for head in range(heads):
            key = turned(total[:, head * 2 * HD : (head * 2 + 1) * HD], 0)
            value = total[:, (head * 2 + 1) * HD : (head * 2 + 2) * HD].astype(BF16)
            out[:, head * 2 * HD : (head * 2 + 1) * HD] = key
            out[:, (head * 2 + 1) * HD : (head * 2 + 2) * HD] = value
            pieces.append(jnp.concatenate([key, value], axis=1).astype(F32))
        mine = pieces[0]
        for head in range(1, heads):
            mine = jnp.where(place_ref[1] == head, pieces[head], mine)
        blocks = [mine]
        for sub in range(1, splits):
            group = other_refs[(sub - 1) * ranks : sub * ranks]
            total = functools.reduce(jnp.add, [ref[...] for ref in group])
            key = turned(total[:, :HD], sub)
            blocks.append(
                jnp.concatenate([key, total[:, HD:].astype(BF16)], axis=1).astype(F32)
            )
        suffix[...] = jnp.concatenate(blocks, axis=0).astype(BF16)

    flat = [array for arrays in others for array in arrays]
    return pl.pallas_call(
        body,
        in_specs=[SMEM] + [VMEM] * (ranks + len(flat) + 2) + [ANY],
        out_specs=[VMEM, VMEM],
        out_shape=[
            jax.ShapeDtypeStruct((rows, heads * 2 * HD), BF16),
            jax.ShapeDtypeStruct((rows * splits, 2 * HD), BF16),
        ],
        compiler_params=params(4),
        cost_estimate=TINY,
    )(place, *own, *flat, cosine, sine, awaited)


def collect_pages(listed, place, sources, pages, splits):
    slots = pages * splits * GROUPS

    def body(list_ref, place_ref, *refs):
        count = len(sources)
        own_keys, own_values, *others = refs[:count]
        keys_out, values_out, key_sem, value_sem = refs[count:]
        here = place_ref[1] * GROUPS + place_ref[0]
        number = list_ref[PLACE]

        def copies(which, page, at):
            rows = pl.ds(pl.multiple_of(at * PAGE, PAGE), PAGE)
            if which:
                views = [others[which - 1].at[kind, page] for kind in range(2)]
            else:
                view = (page, slice(None), pl.ds(pl.multiple_of(place_ref[1] * HD, HD), HD))
                views = [ref.at[view] for ref in (own_keys, own_values)]
            return (
                pltpu.make_async_copy(views[0], keys_out.at[rows], key_sem.at[at]),
                pltpu.make_async_copy(views[1], values_out.at[rows], value_sem.at[at]),
            )

        def begin(i, carry):
            slot = list_ref[PLACE + 1 + i]
            device = slot // pages
            page = slot - device * pages
            kind = jnp.bitwise_xor(device, here)
            for which in range(splits * GROUPS):

                @pl.when(kind == which)
                def _():
                    for copy in copies(which, page, i):
                        copy.start()

            return carry

        lax.fori_loop(0, number, begin, 0)

        def clear(i, carry):
            rows = pl.ds(pl.multiple_of(i * PAGE, PAGE), PAGE)
            values_out[rows, :] = jnp.zeros((PAGE, HD), BF16)
            return carry

        lax.fori_loop(number, jnp.minimum(number + CHUNK - 1, slots), clear, 0)

        def land(i, carry):
            for copy in copies(0, 0, i):
                copy.wait()
            return carry

        lax.fori_loop(0, number, land, 0)

    return pl.pallas_call(
        body,
        in_specs=[SMEM, SMEM] + [ANY] * len(sources),
        out_specs=[VMEM, VMEM],
        out_shape=[
            jax.ShapeDtypeStruct((slots * PAGE, HD), BF16),
            jax.ShapeDtypeStruct((slots * PAGE, HD), BF16),
        ],
        scratch_shapes=[pltpu.SemaphoreType.DMA((slots,)), pltpu.SemaphoreType.DMA((slots,))],
        compiler_params=params(16),
        cost_estimate=TINY,
    )(listed, place, *sources)


def attend(listed, lengths, place, fars, queries, suffix, keys, values, rows_each):
    tokens = queries[0].shape[0]
    splits = tokens // rows_each
    heads = queries[0].shape[1] // HD
    rows = tokens * heads
    slots = keys.shape[0] // PAGE
    wide = CHUNK * PAGE
    parts = -(-rows // HD)
    stat_rows = -(-3 * parts // 16) * 16
    blocks = len(queries)

    def body(list_ref, len_ref, place_ref, *refs):
        query_refs, refs = refs[:blocks], refs[blocks:]
        suffix_ref, keys_ref, values_ref, refs = refs[0], refs[1], refs[2], refs[3:]
        outs, (stacked, top, total, column, stats) = refs[:blocks], refs[blocks:]
        count = list_ref[PLACE]
        turns = lax.div(count + (CHUNK - 1), CHUNK)
        group, split, z_here = place_ref[0], place_ref[1], place_ref[3]

        def places(z, axis):
            index = lax.broadcasted_iota(jnp.int32, (tokens, tokens), axis)
            result = jnp.zeros((tokens, tokens), jnp.int32)
            for sub in range(splits):
                block = z * splits + jnp.bitwise_xor(split, sub)
                result = jnp.where(
                    index >= sub * rows_each, (block - sub) * rows_each + index, result
                )
            return result

        own_keys = suffix_ref[:, :HD]
        own_values = jnp.concatenate([suffix_ref[:, HD:], jnp.ones((tokens, HD), BF16)], axis=1)
        key_place = places(z_here, 1)
        for b in range(blocks):
            q = jnp.concatenate(
                [query_refs[b][:, h * HD : (h + 1) * HD].astype(F32) for h in range(heads)], axis=0
            ).astype(BF16)
            stacked[b] = q
            query_place = places(jnp.bitwise_xor(z_here, fars[b]), 0)
            begins = jnp.zeros((tokens, tokens), jnp.int32)
            edge = jnp.int32(0)
            for r in range(REQS):
                edge = edge + len_ref[group, r]
                begins = jnp.where(query_place >= edge, edge, begins)
            seen = jnp.logical_and(key_place <= query_place, key_place >= begins)
            seen = jnp.concatenate([seen.astype(F32)] * heads, axis=0)
            own = lax.dot_general(q, own_keys, NT, preferred_element_type=F32)
            own = jnp.where(seen > 0.0, own, LOW)
            highest = jnp.max(own, axis=1, keepdims=True)
            weights = jnp.exp2((own - highest) * EXP2_SCALE) * seen
            total[b] = jnp.dot(weights.astype(BF16), own_values, preferred_element_type=F32)
            top[b] = jnp.broadcast_to(highest, (rows, HD))

        def turn(c, carry):
            span = pl.ds(pl.multiple_of(c * wide, wide), wide)
            chunk_keys = keys_ref[span, :]
            chunk_values = jnp.concatenate(
                [values_ref[span, :], jnp.ones((wide, HD), BF16)], axis=1
            )
            found = [
                lax.dot_general(stacked[b], chunk_keys, NT, preferred_element_type=F32)
                for b in range(blocks)
            ]
            for b in range(blocks):
                pieces = [
                    jnp.where(c * CHUNK + j < count, found[b][:, j * PAGE : (j + 1) * PAGE], LOW)
                    for j in range(CHUNK)
                ]
                best = functools.reduce(jnp.maximum, pieces)
                before = top[b]
                highest = jnp.maximum(before, jnp.max(best, axis=1, keepdims=True))
                weights = jnp.concatenate(
                    [jnp.exp2((piece - highest) * EXP2_SCALE).astype(BF16) for piece in pieces],
                    axis=1,
                )
                factor = jnp.exp2((before - highest) * EXP2_SCALE)
                added = jnp.dot(weights, chunk_values, preferred_element_type=F32)
                total[b] = total[b] * jnp.concatenate([factor, factor], axis=1) + added
                top[b] = highest
            return carry

        lax.fori_loop(0, turns, turn, 0)
        for b in range(blocks):
            sums = total[b, :, HD:]
            some = sums > 0.0
            safe = jnp.where(some, sums, 1.0)
            outs[b][0:rows, :] = (total[b, :, :HD] / safe).astype(BF16)
            column[0:rows, :] = jnp.where(some, top[b] * EXP2_SCALE + jnp.log2(safe), LOW)
            stats[...] = jnp.zeros((stat_rows, HD), F32)
            for part in range(parts):
                line = column[part * HD : (part + 1) * HD, :].T[0:1, :]
                for piece in range(3):
                    rounded = line.astype(BF16).astype(F32)
                    stats[3 * part + piece : 3 * part + piece + 1, :] = rounded
                    line = line - rounded
            outs[b][rows : rows + stat_rows, :] = stats[...].astype(BF16)

    return pl.pallas_call(
        body,
        in_specs=[SMEM, SMEM, SMEM] + [VMEM] * (blocks + 3),
        out_specs=[VMEM] * blocks,
        out_shape=[jax.ShapeDtypeStruct((rows + stat_rows, HD), BF16)] * blocks,
        scratch_shapes=[
            pltpu.VMEM((blocks, rows, HD), BF16),
            pltpu.VMEM((blocks, rows, HD), F32),
            pltpu.VMEM((blocks, rows, 2 * HD), F32),
            pltpu.VMEM((parts * HD, HD), F32),
            pltpu.VMEM((stat_rows, HD), F32),
        ],
        compiler_params=params(16),
        cost_estimate=pl.CostEstimate(
            flops=4 * blocks * rows * slots * PAGE * HD,
            bytes_accessed=slots * PAGE * HD * 3,
            transcendentals=blocks * rows * slots * PAGE // 2,
        ),
    )(listed, lengths, place, *queries, suffix, keys, values)


def fetch_rows(weight, place, depth, after):
    def body(place_ref, weight_ref, after_ref, out, sem):
        start = pl.multiple_of(place_ref[1] * depth, depth)
        copy = pltpu.make_async_copy(weight_ref.at[pl.ds(start, depth)], out, sem)
        copy.start()
        copy.wait()

    return pl.pallas_call(
        body,
        in_specs=[SMEM, HBM, ANY],
        out_specs=VMEM,
        out_shape=jax.ShapeDtypeStruct((depth, weight.shape[1]), BF16),
        scratch_shapes=[pltpu.SemaphoreType.DMA],
        compiler_params=params(40),
        cost_estimate=pl.CostEstimate(
            flops=0, bytes_accessed=4 * depth * weight.shape[1], transcendentals=0
        ),
    )(place, weight, after)


def project(place, partials, weight, rows_each, splits, ranks, heads):
    tokens = rows_each * splits
    rows = tokens * heads
    parts = -(-rows // HD)
    width = weight.shape[1] // ranks

    def body(place_ref, *refs):
        count = len(partials)
        partial_refs, weight_ref, outs = refs[:count], refs[count], refs[count + 1 : -2]
        merged, attended = refs[-2:]
        for part in range(parts):
            length = min(HD, rows - part * HD)
            lines = []
            for ref in partial_refs:
                stat = ref[rows:, :].astype(F32)
                lines.append(
                    stat[3 * part : 3 * part + 1]
                    + stat[3 * part + 1 : 3 * part + 2]
                    + stat[3 * part + 2 : 3 * part + 3]
                )
            best = functools.reduce(jnp.maximum, lines)
            shares = [jnp.exp2(line - best) for line in lines]
            whole = functools.reduce(jnp.add, shares)
            mixed = jnp.zeros((length, HD), F32)
            for share, ref in zip(shares, partial_refs):
                factor = jnp.broadcast_to(share / whole, (HD, HD)).T[:length]
                mixed = mixed + factor * ref[part * HD : part * HD + length, :].astype(F32)
            merged[part * HD : part * HD + length, :] = mixed
        for h in range(heads):
            attended[:, h * HD : (h + 1) * HD] = merged[h * tokens : (h + 1) * tokens, :].astype(
                BF16
            )
        for rank in range(ranks):
            start = pl.multiple_of(jnp.bitwise_xor(place_ref[4], rank) * width, width)
            product = jnp.dot(
                attended[...], weight_ref[:, pl.ds(start, width)], preferred_element_type=F32
            )
            for sub in range(splits):
                out = outs[rank * splits + sub]
                out[...] = product[sub * rows_each : (sub + 1) * rows_each].astype(out.dtype)

    return pl.pallas_call(
        body,
        in_specs=[SMEM] + [VMEM] * (len(partials) + 1),
        out_specs=[VMEM] * (ranks * splits),
        out_shape=[
            jax.ShapeDtypeStruct((rows_each, width), BF16 if i else F32)
            for i in range(ranks * splits)
        ],
        scratch_shapes=[pltpu.VMEM((rows, HD), F32), pltpu.VMEM((tokens, heads * HD), BF16)],
        compiler_params=params(16),
        cost_estimate=pl.CostEstimate(
            flops=2 * tokens * weight.size, bytes_accessed=weight.size, transcendentals=0
        ),
    )(place, *partials, weight)


def local(
    hidden_in,
    kv_weight,
    queries,
    prefix_keys,
    prefix_values,
    page_table,
    suffix_lengths,
    out_weight,
):
    rows = hidden_in.shape[0]
    seq_count, ranks = lax.axis_size("seq"), lax.axis_size("tp")
    seq_rank, tp_rank = lax.axis_index("seq"), lax.axis_index("tp")
    pages = prefix_keys.shape[0]
    splits = prefix_keys.shape[2] // HD
    heads = queries.shape[1] // HD // splits
    prefix_len = pages * seq_count // GROUPS * PAGE
    blocks = seq_count // GROUPS
    depth = blocks // splits
    group = seq_rank % GROUPS
    block = seq_rank // GROUPS
    split = block % splits
    place = jnp.stack(
        [group, split, (block - split) * GROUPS * pages, block // splits, tp_rank]
    ).astype(jnp.int32)

    def across(array, far=0, side=0, core=0):
        step = (far * splits + side) * GROUPS + core
        return lax.ppermute(array, "seq", [(i, i ^ step) for i in range(seq_count)])

    def columns(array, index, width):
        return lax.dynamic_slice_in_dim(array, index * width, width, 1)

    def quad(array, rank, side):
        step = side * GROUPS
        route = [
            (i * ranks + j, (i ^ step) * ranks + (j ^ rank))
            for i in range(seq_count)
            for j in range(ranks)
        ]
        return lax.ppermute(array, ("seq", "tp"), route)

    def columns(array, index, width):
        return lax.dynamic_slice_in_dim(array, index * width, width, array.ndim - 1)

    parts = [columns(queries, split, heads * HD)]
    for side in range(1, splits):
        parts.append(across(columns(queries, split ^ side, heads * HD), side=side))
    my_query = jnp.concatenate(parts, axis=0)
    listed = list_pages(page_table, place, pages, splits, my_query)
    far_queries = [my_query] + [across(my_query, far=far) for far in range(1, depth)]
    sent = [
        jnp.stack([columns(array, split ^ side, HD) for array in (prefix_keys, prefix_values)])
        for side in range(splits)
    ]
    arrived = [across(sent[side], side=side) for side in range(1, splits)]
    sources = [prefix_keys, prefix_values, across(sent[0], core=1)]

    projected = project_kv(hidden_in, kv_weight, listed, ranks, splits)
    own = [projected[0]] + [quad(projected[rank * splits], rank, 0) for rank in range(1, ranks)]
    others = [
        [quad(projected[rank * splits + side], rank, side) for rank in range(ranks)]
        for side in range(1, splits)
    ]
    for array in arrived:
        array = array_after(array, projected[0], *far_queries[1:])
        sources += [array, across(array, core=1)]
    keys, values = collect_pages(listed, place, sources, pages, splits)
    lengths = jnp.sum(
        jnp.where(jnp.arange(GROUPS)[:, None] == group, suffix_lengths, 0), axis=0
    )
    ends = jnp.sum(
        jnp.where(jnp.arange(REQS)[None, :] <= jnp.arange(REQS)[:, None], lengths[None, :], 0),
        axis=1,
    )
    index = jnp.arange(rows * splits, dtype=jnp.int32)
    within = (block - split + (split ^ (index // rows))) * rows + index % rows
    begins = jnp.max(jnp.where(within[:, None] >= ends[None, :], ends[None, :], 0), axis=1)
    positions = prefix_len + within - begins
    half = HD // 2
    frequency = jnp.power(500000.0, -(jnp.arange(half, dtype=F32) * 2.0 / HD))
    angles = positions.astype(F32)[:, None] * frequency[None, :]
    cosine, sine = jnp.cos(angles), jnp.sin(angles)
    cosine = jnp.concatenate([cosine, cosine], axis=1)
    sine = jnp.concatenate([-sine, sine], axis=1)
    new_pages, suffix = finish_kv(place, own, others, cosine, sine, splits, keys)

    returned = []
    order = list(range(depth - 1, -1, -1))
    for first in range(0, depth, BLOCKS):
        fars = order[first : first + BLOCKS]
        sums = attend(
            listed, suffix_lengths, place, fars, [far_queries[far] for far in fars],
            suffix, keys, values, rows,
        )
        returned += [across(part, far=far) if far else part for far, part in zip(fars, sums)]

    weight = fetch_rows(out_weight, place, heads * HD, returned[-1])
    products = project(place, returned, weight, rows, splits, ranks, heads)
    hidden = products[0]
    for rank in range(ranks - 1, -1, -1):
        for side in range(splits - 1, -1, -1):
            if rank or side:
                hidden = hidden + quad(products[rank * splits + side], rank, side).astype(F32)
    return (hidden.astype(BF16), new_pages)


def solution(mesh):
    return jax.shard_map(
        local,
        mesh=mesh,
        in_specs=(
            P("seq", "tp"),
            P("tp", None),
            P("seq", "tp"),
            P("seq", None, "tp"),
            P("seq", None, "tp"),
            P(),
            P(),
            P("tp", None),
        ),
        out_specs=(P("seq", "tp"), P("seq", "tp")),
        check_vma=False,
    )
```

```python
import functools
import math

import jax
import jax.numpy as jnp
from jax import lax
from jax.experimental import pallas as pl
from jax.experimental.pallas import tpu as pltpu
from jax.sharding import PartitionSpec as P

HD = 128
PAGE = 128
GROUPS = 2
REQS = 8
PLACE = 5
CHUNK = 4
BLOCKS = 2
AHEAD = 8
LOW = -1e30
EXP2_SCALE = math.log2(math.e) / math.sqrt(HD)
F32 = jnp.float32
BF16 = jnp.bfloat16
MIB = 1 << 20

NT = (((1,), (1,)), ((), ()))

VMEM = pl.BlockSpec(memory_space=pltpu.VMEM)
SMEM = pl.BlockSpec(memory_space=pltpu.SMEM)
ANY = pl.BlockSpec(memory_space=pl.ANY)
HBM = pl.BlockSpec(memory_space=pltpu.HBM)


TINY = pl.CostEstimate(flops=1, bytes_accessed=1, transcendentals=0)


def params(mib):
    return pltpu.CompilerParams(vmem_limit_bytes=mib * MIB)


def array_after(array, *awaited):
    def body(*refs):
        pass

    return pl.pallas_call(
        body,
        in_specs=[ANY] * (1 + len(awaited)),
        out_specs=ANY,
        out_shape=jax.ShapeDtypeStruct(array.shape, array.dtype),
        input_output_aliases={0: 0},
        compiler_params=params(2),
        cost_estimate=TINY,
    )(array, *awaited)


def project_kv(hidden_in, weight, table, ranks, slots, awaited):
    group_pages = (table.shape[0] - PLACE) // GROUPS
    rows, deep = hidden_in.shape
    width = weight.shape[1] // ranks
    steps = 8
    part = deep // steps

    def body(place_ref, hidden_ref, weight_ref, _, *refs):
        outs, (listed, buffer, sums, sem) = refs[:ranks], refs[ranks:]
        copies = [
            pltpu.make_async_copy(weight_ref.at[pl.ds(i * part, part)], buffer.at[i], sem.at[i])
            for i in range(steps)
        ]
        for copy in copies[:AHEAD]:
            copy.start()
        group, first = place_ref[0], place_ref[2]

        def look(i, number):
            slot = place_ref[PLACE + group * group_pages + i] - first
            here = jnp.logical_and(slot >= 0, slot < slots)
            listed[number + 1] = slot
            return number + here.astype(jnp.int32)

        listed[0] = lax.fori_loop(0, group_pages, look, jnp.int32(0), unroll=8)
        for i, copy in enumerate(copies):
            copy.wait()
            if i + AHEAD < steps:
                copies[i + AHEAD].start()
            product = jnp.dot(
                hidden_ref[:, i * part : (i + 1) * part],
                buffer[i],
                preferred_element_type=F32,
            )
            sums[...] = product if i == 0 else sums[...] + product
        for rank, out in enumerate(outs):
            start = pl.multiple_of(jnp.bitwise_xor(place_ref[4], rank) * width, width)
            out[...] = sums[:, pl.ds(start, width)]

    return pl.pallas_call(
        body,
        in_specs=[SMEM, VMEM, HBM, ANY],
        out_specs=[VMEM] * ranks + [SMEM],
        out_shape=[jax.ShapeDtypeStruct((rows, width), F32)] * ranks
        + [jax.ShapeDtypeStruct((slots + 2,), jnp.int32)],
        scratch_shapes=[
            pltpu.VMEM((steps, part, weight.shape[1]), BF16),
            pltpu.VMEM((rows, weight.shape[1]), F32),
            pltpu.SemaphoreType.DMA((steps,)),
        ],
        compiler_params=params(48),
        cost_estimate=TINY,
    )(table, hidden_in, weight, awaited)


def finish_kv(place, mine, others, cosine, sine, heads):
    rows = mine.shape[0]

    def body(place_ref, *refs):
        count = 1 + len(others)
        out, pieces = refs[count + 2], refs[count + 3 :]
        total = refs[0][...]
        for other in refs[1:count]:
            total = total + other[...]
        cos, sin = refs[count][...], refs[count + 1][...]
        for head in range(heads):
            key = total[:, head * 2 * HD : (head * 2 + 1) * HD]
            key = (key * cos + pltpu.roll(key, HD // 2, 1) * sin).astype(BF16)
            value = total[:, (head * 2 + 1) * HD : (head * 2 + 2) * HD].astype(BF16)
            out[:, head * 2 * HD : (head * 2 + 1) * HD] = key
            out[:, (head * 2 + 1) * HD : (head * 2 + 2) * HD] = value
            for step in range(heads):

                @pl.when(jnp.bitwise_xor(place_ref[1], step) == head)
                def _():
                    pieces[step][:, :HD] = key
                    pieces[step][:, HD:] = value

    return pl.pallas_call(
        body,
        in_specs=[SMEM] + [VMEM] * (3 + len(others)),
        out_specs=[VMEM] * (1 + heads),
        out_shape=[jax.ShapeDtypeStruct((rows, heads * 2 * HD), BF16)]
        + [jax.ShapeDtypeStruct((rows, 2 * HD), BF16)] * heads,
        compiler_params=params(4),
        cost_estimate=TINY,
    )(place, mine, *others, cosine, sine)


def collect_pages(listed, place, sources, pages, splits):
    slots = pages * splits * GROUPS

    def body(list_ref, place_ref, *refs):
        own_keys, own_values, *others = refs[: len(sources)]
        keys_out, values_out = refs[len(sources) :]
        here = place_ref[1] * GROUPS + place_ref[0]
        number = list_ref[0]

        def rows(i):
            return pl.ds(pl.multiple_of(i * PAGE, PAGE), PAGE)

        def collect(i, carry):
            slot = list_ref[1 + i]
            device = slot // pages
            page = slot - device * pages
            kind = jnp.bitwise_xor(device, here)

            @pl.when(kind == 0)
            def _():
                column = pl.ds(pl.multiple_of(place_ref[1] * HD, HD), HD)
                keys_out[rows(i), :] = own_keys[page, :, column]
                values_out[rows(i), :] = own_values[page, :, column]

            for which, other in enumerate(others):

                @pl.when(kind == which + 1)
                def _():
                    keys_out[rows(i), :] = other[0, page]
                    values_out[rows(i), :] = other[1, page]

            return carry

        lax.fori_loop(0, number, collect, 0)

        def clear(i, carry):
            values_out[rows(i), :] = jnp.zeros((PAGE, HD), BF16)
            return carry

        lax.fori_loop(number, jnp.minimum(number + CHUNK - 1, slots), clear, 0)

    return pl.pallas_call(
        body,
        in_specs=[SMEM, SMEM] + [VMEM] * len(sources),
        out_specs=[VMEM, VMEM],
        out_shape=[
            jax.ShapeDtypeStruct((slots * PAGE, HD), BF16),
            jax.ShapeDtypeStruct((slots * PAGE, HD), BF16),
        ],
        compiler_params=params(16),
        cost_estimate=TINY,
    )(listed, place, *sources)


def attend(listed, lengths, place, fars, queries, suffix, keys, values, rows_each, weight=None):
    fetched = [] if weight is None else [weight]
    tokens = queries[0].shape[0]
    splits = tokens // rows_each
    heads = queries[0].shape[1] // HD
    rows = tokens * heads
    slots = keys.shape[0] // PAGE
    wide = CHUNK * PAGE
    parts = -(-rows // HD)
    stat_rows = -(-3 * parts // 16) * 16
    blocks = len(queries)

    def body(list_ref, len_ref, place_ref, *refs):
        if fetched:
            weight_ref, rows_out, weight_sem = refs[0], refs[-8], refs[-1]
            refs = (*refs[1:-8], *refs[-7:-1])
            start = pl.multiple_of(place_ref[1] * heads * HD, heads * HD)
            copy = pltpu.make_async_copy(
                weight_ref.at[pl.ds(start, heads * HD)], rows_out, weight_sem
            )
            copy.start()
        query_refs, refs = refs[:blocks], refs[blocks:]
        suffix_refs, refs = refs[:splits], refs[splits:]
        keys_ref, values_ref, refs = refs[0], refs[1], refs[2:]
        outs, (stacked, scores, top, total, column, stats) = refs[:blocks], refs[blocks:]
        count = list_ref[0]
        turns = lax.div(count + (CHUNK - 1), CHUNK)
        group, split, z_here = place_ref[0], place_ref[1], place_ref[3]

        def places(z, axis):
            index = lax.broadcasted_iota(jnp.int32, (tokens, tokens), axis)
            result = jnp.zeros((tokens, tokens), jnp.int32)
            for sub in range(splits):
                block = z * splits + jnp.bitwise_xor(split, sub)
                result = jnp.where(
                    index >= sub * rows_each, (block - sub) * rows_each + index, result
                )
            return result

        own_kv = jnp.concatenate([ref[...].astype(F32) for ref in suffix_refs], axis=0).astype(BF16)
        own_keys = own_kv[:, :HD]
        own_values = jnp.concatenate([own_kv[:, HD:], jnp.ones((tokens, HD), BF16)], axis=1)
        key_place = places(z_here, 1)
        for b in range(blocks):
            q = jnp.concatenate(
                [query_refs[b][:, h * HD : (h + 1) * HD].astype(F32) for h in range(heads)], axis=0
            ).astype(BF16)
            stacked[b] = q
            query_place = places(jnp.bitwise_xor(z_here, fars[b]), 0)
            begins = jnp.zeros((tokens, tokens), jnp.int32)
            edge = jnp.int32(0)
            for r in range(REQS):
                edge = edge + len_ref[group, r]
                begins = jnp.where(query_place >= edge, edge, begins)
            seen = jnp.logical_and(key_place <= query_place, key_place >= begins)
            seen = jnp.concatenate([seen.astype(F32)] * heads, axis=0)
            own = lax.dot_general(q, own_keys, NT, preferred_element_type=F32)
            own = jnp.where(seen > 0.0, own, LOW)
            highest = jnp.max(own, axis=1, keepdims=True)
            weights = jnp.exp2((own - highest) * EXP2_SCALE) * seen
            total[b] = jnp.dot(weights.astype(BF16), own_values, preferred_element_type=F32)
            top[b] = jnp.broadcast_to(highest, (rows, HD))

        def score(b, c):
            span = pl.ds(pl.multiple_of(c * wide, wide), wide)
            scores[b] = lax.dot_general(
                stacked[b], keys_ref[span, :], NT, preferred_element_type=F32
            )

        def turn(c, carry):
            span = pl.ds(pl.multiple_of(c * wide, wide), wide)
            chunk_values = jnp.concatenate(
                [values_ref[span, :], jnp.ones((wide, HD), BF16)], axis=1
            )
            for b in range(blocks):
                pieces = [
                    jnp.where(c * CHUNK + j < count, scores[b, :, j * PAGE : (j + 1) * PAGE], LOW)
                    for j in range(CHUNK)
                ]
                best = functools.reduce(jnp.maximum, pieces)
                before = top[b]
                highest = jnp.maximum(before, jnp.max(best, axis=1, keepdims=True))
                weights = jnp.concatenate(
                    [jnp.exp2((piece - highest) * EXP2_SCALE).astype(BF16) for piece in pieces],
                    axis=1,
                )
                factor = jnp.exp2((before - highest) * EXP2_SCALE)
                added = jnp.dot(weights, chunk_values, preferred_element_type=F32)
                total[b] = total[b] * jnp.concatenate([factor, factor], axis=1) + added
                top[b] = highest
                score(b, jnp.minimum(c + 1, slots // CHUNK - 1))
            return carry

        for b in range(blocks):
            score(b, 0)
        lax.fori_loop(0, turns, turn, 0)
        for b in range(blocks):
            sums = total[b, :, HD:]
            some = sums > 0.0
            safe = jnp.where(some, sums, 1.0)
            outs[b][0:rows, :] = (total[b, :, :HD] / safe).astype(BF16)
            column[0:rows, :] = jnp.where(some, top[b] * EXP2_SCALE + jnp.log2(safe), LOW)
            stats[...] = jnp.zeros((stat_rows, HD), F32)
            for part in range(parts):
                line = column[part * HD : (part + 1) * HD, :].T[0:1, :]
                for piece in range(3):
                    rounded = line.astype(BF16).astype(F32)
                    stats[3 * part + piece : 3 * part + piece + 1, :] = rounded
                    line = line - rounded
            outs[b][rows : rows + stat_rows, :] = stats[...].astype(BF16)
        if fetched:
            copy.wait()

    return pl.pallas_call(
        body,
        in_specs=[SMEM, SMEM, SMEM] + [HBM] * len(fetched) + [VMEM] * (blocks + splits + 2),
        out_specs=[VMEM] * blocks + [ANY] * len(fetched),
        out_shape=[jax.ShapeDtypeStruct((rows + stat_rows, HD), BF16)] * blocks
        + [jax.ShapeDtypeStruct((heads * HD, array.shape[1]), BF16) for array in fetched],
        scratch_shapes=[
            pltpu.VMEM((blocks, rows, HD), BF16),
            pltpu.VMEM((blocks, rows, wide), F32),
            pltpu.VMEM((blocks, rows, HD), F32),
            pltpu.VMEM((blocks, rows, 2 * HD), F32),
            pltpu.VMEM((parts * HD, HD), F32),
            pltpu.VMEM((stat_rows, HD), F32),
        ]
        + [pltpu.SemaphoreType.DMA] * len(fetched),
        compiler_params=params(40 if fetched else 16),
        cost_estimate=pl.CostEstimate(
            flops=4 * blocks * rows * slots * PAGE * HD,
            bytes_accessed=slots * PAGE * HD * 3,
            transcendentals=blocks * rows * slots * PAGE // 2,
        ),
    )(listed, lengths, place, *fetched, *queries, *suffix, keys, values)


def project(place, partials, weight, rows_each, splits, ranks, heads):
    tokens = rows_each * splits
    rows = tokens * heads
    parts = -(-rows // HD)
    width = weight.shape[1] // ranks

    def body(place_ref, *refs):
        count = len(partials)
        partial_refs, weight_ref, outs = refs[:count], refs[count], refs[count + 1 : -2]
        merged, attended = refs[-2:]
        for part in range(parts):
            length = min(HD, rows - part * HD)
            lines = []
            for ref in partial_refs:
                stat = ref[rows:, :].astype(F32)
                lines.append(
                    stat[3 * part : 3 * part + 1]
                    + stat[3 * part + 1 : 3 * part + 2]
                    + stat[3 * part + 2 : 3 * part + 3]
                )
            best = functools.reduce(jnp.maximum, lines)
            shares = [jnp.exp2(line - best) for line in lines]
            whole = functools.reduce(jnp.add, shares)
            mixed = jnp.zeros((length, HD), F32)
            for share, ref in zip(shares, partial_refs):
                factor = jnp.broadcast_to(share / whole, (HD, HD)).T[:length]
                mixed = mixed + factor * ref[part * HD : part * HD + length, :].astype(F32)
            merged[part * HD : part * HD + length, :] = mixed
        for h in range(heads):
            attended[:, h * HD : (h + 1) * HD] = merged[h * tokens : (h + 1) * tokens, :].astype(
                BF16
            )
        for rank in range(ranks):
            start = pl.multiple_of(jnp.bitwise_xor(place_ref[4], rank) * width, width)
            product = jnp.dot(
                attended[...], weight_ref[:, pl.ds(start, width)], preferred_element_type=F32
            )
            for sub in range(splits):
                out = outs[rank * splits + sub]
                out[...] = product[sub * rows_each : (sub + 1) * rows_each].astype(out.dtype)

    return pl.pallas_call(
        body,
        in_specs=[SMEM] + [VMEM] * (len(partials) + 1),
        out_specs=[VMEM] * (ranks * splits),
        out_shape=[
            jax.ShapeDtypeStruct((rows_each, width), BF16 if i else F32)
            for i in range(ranks * splits)
        ],
        scratch_shapes=[pltpu.VMEM((rows, HD), F32), pltpu.VMEM((tokens, heads * HD), BF16)],
        compiler_params=params(16),
        cost_estimate=pl.CostEstimate(
            flops=2 * tokens * weight.size, bytes_accessed=weight.size, transcendentals=0
        ),
    )(place, *partials, weight)


def local(
    hidden_in,
    kv_weight,
    queries,
    prefix_keys,
    prefix_values,
    page_table,
    suffix_lengths,
    out_weight,
):
    rows = hidden_in.shape[0]
    seq_count, ranks = lax.axis_size("seq"), lax.axis_size("tp")
    seq_rank, tp_rank = lax.axis_index("seq"), lax.axis_index("tp")
    pages = prefix_keys.shape[0]
    splits = prefix_keys.shape[2] // HD
    heads = queries.shape[1] // HD // splits
    prefix_len = pages * seq_count // GROUPS * PAGE
    blocks = seq_count // GROUPS
    depth = blocks // splits
    group = seq_rank % GROUPS
    block = seq_rank // GROUPS
    split = block % splits
    place = jnp.stack(
        [group, split, (block - split) * GROUPS * pages, block // splits, tp_rank]
    ).astype(jnp.int32)
    place = jnp.concatenate([place, page_table])

    def across(array, far=0, side=0, core=0):
        step = (far * splits + side) * GROUPS + core
        return lax.ppermute(array, "seq", [(i, i ^ step) for i in range(seq_count)])

    def columns(array, index, width):
        return lax.dynamic_slice_in_dim(array, index * width, width, 1)

    def quad(array, rank, side):
        step = side * GROUPS
        route = [
            (i * ranks + j, (i ^ step) * ranks + (j ^ rank))
            for i in range(seq_count)
            for j in range(ranks)
        ]
        return lax.ppermute(array, ("seq", "tp"), route)

    def columns(array, index, width):
        return lax.dynamic_slice_in_dim(array, index * width, width, array.ndim - 1)

    parts = [columns(queries, split, heads * HD)]
    for side in range(1, splits):
        parts.append(across(columns(queries, split ^ side, heads * HD), side=side))
    my_query = jnp.concatenate(parts, axis=0)
    far_queries = [my_query] + [across(my_query, far=far) for far in range(1, depth)]
    sent = [
        jnp.stack([columns(array, split ^ side, HD) for array in (prefix_keys, prefix_values)])
        for side in range(splits)
    ]
    arrived = [across(sent[side], side=side) for side in range(1, splits)]
    sources = [prefix_keys, prefix_values, across(sent[0], core=1)]

    *projected, listed = project_kv(
        hidden_in, kv_weight, place, ranks, pages * splits * GROUPS, my_query
    )
    others = [
        lax.ppermute(projected[rank], "tp", [(i, i ^ rank) for i in range(ranks)])
        for rank in range(1, ranks)
    ]
    lengths = jnp.sum(
        jnp.where(jnp.arange(GROUPS)[:, None] == group, suffix_lengths, 0), axis=0
    )
    ends = jnp.sum(
        jnp.where(jnp.arange(REQS)[None, :] <= jnp.arange(REQS)[:, None], lengths[None, :], 0),
        axis=1,
    )
    within = block * rows + jnp.arange(rows, dtype=jnp.int32)
    begins = jnp.max(jnp.where(within[:, None] >= ends[None, :], ends[None, :], 0), axis=1)
    positions = prefix_len + within - begins
    half = HD // 2
    frequency = jnp.power(500000.0, -(jnp.arange(half, dtype=F32) * 2.0 / HD))
    angles = positions.astype(F32)[:, None] * frequency[None, :]
    cosine, sine = jnp.cos(angles), jnp.sin(angles)
    cosine = jnp.concatenate([cosine, cosine], axis=1)
    sine = jnp.concatenate([-sine, sine], axis=1)
    new_pages, *suffix = finish_kv(place, projected[0], others, cosine, sine, splits)
    suffix = suffix[:1] + [across(suffix[side], side=side) for side in range(1, splits)]

    for array in arrived:
        array = array_after(array, *others, *far_queries[1:])
        sources += [array, across(array, core=1)]
    keys, values = collect_pages(listed, place, sources, pages, splits)

    returned = []
    order = list(range(depth - 1, -1, -1))
    calls = [order[i : i + BLOCKS] for i in range(0, depth - BLOCKS, BLOCKS)]
    calls += [[far] for far in order[len(calls) * BLOCKS :]]
    for i, fars in enumerate(calls):
        sums = attend(
            listed, suffix_lengths, place, fars, [far_queries[far] for far in fars],
            suffix, keys, values, rows, None if i else out_weight,
        )
        if not i:
            weight = sums[-1]
        returned += [across(part, far=far) if far else part for far, part in zip(fars, sums)]

    products = project(place, returned, weight, rows, splits, ranks, heads)
    hidden = products[0]
    for rank in range(ranks - 1, -1, -1):
        for side in range(splits - 1, -1, -1):
            if rank or side:
                hidden = hidden + quad(products[rank * splits + side], rank, side).astype(F32)
    return (hidden.astype(BF16), new_pages)


def solution(mesh):
    return jax.shard_map(
        local,
        mesh=mesh,
        in_specs=(
            P("seq", "tp"),
            P("tp", None),
            P("seq", "tp"),
            P("seq", None, "tp"),
            P("seq", None, "tp"),
            P(),
            P(),
            P("tp", None),
        ),
        out_specs=(P("seq", "tp"), P("seq", "tp")),
        check_vma=False,
    )
```

```python
import functools
import math

import jax
import jax.numpy as jnp
from jax import lax
from jax.experimental import pallas as pl
from jax.experimental.pallas import tpu as pltpu
from jax.sharding import PartitionSpec as P

HD = 128
PAGE = 128
GROUPS = 2
REQS = 8
PLACE = 5
CHUNK = 4
BLOCKS = 2
AHEAD = 8
LOW = -1e30
EXP2_SCALE = math.log2(math.e) / math.sqrt(HD)
F32 = jnp.float32
BF16 = jnp.bfloat16
MIB = 1 << 20

NT = (((1,), (1,)), ((), ()))

VMEM = pl.BlockSpec(memory_space=pltpu.VMEM)
SMEM = pl.BlockSpec(memory_space=pltpu.SMEM)
ANY = pl.BlockSpec(memory_space=pl.ANY)
HBM = pl.BlockSpec(memory_space=pltpu.HBM)


TINY = pl.CostEstimate(flops=1, bytes_accessed=1, transcendentals=0)


def params(mib):
    return pltpu.CompilerParams(vmem_limit_bytes=mib * MIB)


def array_after(array, *awaited):
    def body(*refs):
        pass

    return pl.pallas_call(
        body,
        in_specs=[ANY] * (1 + len(awaited)),
        out_specs=ANY,
        out_shape=jax.ShapeDtypeStruct(array.shape, array.dtype),
        input_output_aliases={0: 0},
        compiler_params=params(2),
        cost_estimate=TINY,
    )(array, *awaited)


def project_kv(hidden_in, weight, table, ranks, slots, awaited):
    group_pages = (table.shape[0] - PLACE) // GROUPS
    rows, deep = hidden_in.shape
    width = weight.shape[1] // ranks
    steps = 8
    part = deep // steps

    def body(place_ref, hidden_ref, weight_ref, _, *refs):
        outs, (listed, buffer, sums, sem) = refs[:ranks], refs[ranks:]
        copies = [
            pltpu.make_async_copy(weight_ref.at[pl.ds(i * part, part)], buffer.at[i], sem.at[i])
            for i in range(steps)
        ]
        for copy in copies[:AHEAD]:
            copy.start()
        group, first = place_ref[0], place_ref[2]

        def look(i, number):
            slot = place_ref[PLACE + group * group_pages + i] - first
            here = jnp.logical_and(slot >= 0, slot < slots)
            listed[number + 1] = slot
            return number + here.astype(jnp.int32)

        listed[0] = lax.fori_loop(0, group_pages, look, jnp.int32(0), unroll=8)
        for i, copy in enumerate(copies):
            copy.wait()
            if i + AHEAD < steps:
                copies[i + AHEAD].start()
            product = jnp.dot(
                hidden_ref[:, i * part : (i + 1) * part],
                buffer[i],
                preferred_element_type=F32,
            )
            sums[...] = product if i == 0 else sums[...] + product
        for rank, out in enumerate(outs):
            start = pl.multiple_of(jnp.bitwise_xor(place_ref[4], rank) * width, width)
            out[...] = sums[:, pl.ds(start, width)]

    return pl.pallas_call(
        body,
        in_specs=[SMEM, VMEM, HBM, ANY],
        out_specs=[VMEM] * ranks + [SMEM],
        out_shape=[jax.ShapeDtypeStruct((rows, width), F32)] * ranks
        + [jax.ShapeDtypeStruct((slots + 2,), jnp.int32)],
        scratch_shapes=[
            pltpu.VMEM((steps, part, weight.shape[1]), BF16),
            pltpu.VMEM((rows, weight.shape[1]), F32),
            pltpu.SemaphoreType.DMA((steps,)),
        ],
        compiler_params=params(48),
        cost_estimate=TINY,
    )(table, hidden_in, weight, awaited)


def finish_kv(place, mine, others, cosine, sine, heads):
    rows = mine.shape[0]

    def body(place_ref, *refs):
        count = 1 + len(others)
        out, pieces = refs[count + 2], refs[count + 3 :]
        total = refs[0][...]
        for other in refs[1:count]:
            total = total + other[...]
        cos, sin = refs[count][...], refs[count + 1][...]
        for head in range(heads):
            key = total[:, head * 2 * HD : (head * 2 + 1) * HD]
            key = (key * cos + pltpu.roll(key, HD // 2, 1) * sin).astype(BF16)
            value = total[:, (head * 2 + 1) * HD : (head * 2 + 2) * HD].astype(BF16)
            out[:, head * 2 * HD : (head * 2 + 1) * HD] = key
            out[:, (head * 2 + 1) * HD : (head * 2 + 2) * HD] = value
            for step in range(heads):

                @pl.when(jnp.bitwise_xor(place_ref[1], step) == head)
                def _():
                    pieces[step][:, :HD] = key
                    pieces[step][:, HD:] = value

    return pl.pallas_call(
        body,
        in_specs=[SMEM] + [VMEM] * (3 + len(others)),
        out_specs=[VMEM] * (1 + heads),
        out_shape=[jax.ShapeDtypeStruct((rows, heads * 2 * HD), BF16)]
        + [jax.ShapeDtypeStruct((rows, 2 * HD), BF16)] * heads,
        compiler_params=params(4),
        cost_estimate=TINY,
    )(place, mine, *others, cosine, sine)


def collect_pages(listed, place, sources, pages, splits):
    slots = pages * splits * GROUPS

    def body(list_ref, place_ref, *refs):
        own_keys, own_values, *others = refs[: len(sources)]
        keys_out, values_out = refs[len(sources) :]
        here = place_ref[1] * GROUPS + place_ref[0]
        number = list_ref[0]

        def rows(i):
            return pl.ds(pl.multiple_of(i * PAGE, PAGE), PAGE)

        def collect(i, carry):
            slot = list_ref[1 + i]
            device = slot // pages
            page = slot - device * pages
            kind = jnp.bitwise_xor(device, here)

            @pl.when(kind == 0)
            def _():
                column = pl.ds(pl.multiple_of(place_ref[1] * HD, HD), HD)
                keys_out[rows(i), :] = own_keys[page, :, column]
                values_out[rows(i), :] = own_values[page, :, column]

            for which, other in enumerate(others):

                @pl.when(kind == which + 1)
                def _():
                    keys_out[rows(i), :] = other[0, page]
                    values_out[rows(i), :] = other[1, page]

            return carry

        lax.fori_loop(0, number, collect, 0)

        def clear(i, carry):
            values_out[rows(i), :] = jnp.zeros((PAGE, HD), BF16)
            return carry

        lax.fori_loop(number, jnp.minimum(number + CHUNK - 1, slots), clear, 0)

    return pl.pallas_call(
        body,
        in_specs=[SMEM, SMEM] + [VMEM] * len(sources),
        out_specs=[VMEM, VMEM],
        out_shape=[
            jax.ShapeDtypeStruct((slots * PAGE, HD), BF16),
            jax.ShapeDtypeStruct((slots * PAGE, HD), BF16),
        ],
        compiler_params=params(16),
        cost_estimate=TINY,
    )(listed, place, *sources)


def attend(listed, lengths, place, fars, queries, suffix, keys, values, rows_each, weight=None):
    fetched = [] if weight is None else [weight]
    tokens = queries[0].shape[0]
    splits = tokens // rows_each
    heads = queries[0].shape[1] // HD
    rows = tokens * heads
    slots = keys.shape[0] // PAGE
    wide = CHUNK * PAGE
    parts = -(-rows // HD)
    stat_rows = -(-3 * parts // 16) * 16
    blocks = len(queries)

    def body(list_ref, len_ref, place_ref, *refs):
        if fetched:
            weight_ref, rows_out, weight_sem = refs[0], refs[-8], refs[-1]
            refs = (*refs[1:-8], *refs[-7:-1])
            start = pl.multiple_of(place_ref[1] * heads * HD, heads * HD)
            copy = pltpu.make_async_copy(
                weight_ref.at[pl.ds(start, heads * HD)], rows_out, weight_sem
            )
            copy.start()
        query_refs, refs = refs[:blocks], refs[blocks:]
        suffix_refs, refs = refs[:splits], refs[splits:]
        keys_ref, values_ref, refs = refs[0], refs[1], refs[2:]
        outs, (stacked, scores, top, total, column, stats) = refs[:blocks], refs[blocks:]
        count = list_ref[0]
        turns = lax.div(count + (CHUNK - 1), CHUNK)
        group, split, z_here = place_ref[0], place_ref[1], place_ref[3]

        def places(z, axis):
            index = lax.broadcasted_iota(jnp.int32, (tokens, tokens), axis)
            result = jnp.zeros((tokens, tokens), jnp.int32)
            for sub in range(splits):
                block = z * splits + jnp.bitwise_xor(split, sub)
                result = jnp.where(
                    index >= sub * rows_each, (block - sub) * rows_each + index, result
                )
            return result

        own_kv = jnp.concatenate([ref[...].astype(F32) for ref in suffix_refs], axis=0).astype(BF16)
        own_keys = own_kv[:, :HD]
        own_values = jnp.concatenate([own_kv[:, HD:], jnp.ones((tokens, HD), BF16)], axis=1)
        key_place = places(z_here, 1)
        for b in range(blocks):
            q = jnp.concatenate(
                [query_refs[b][:, h * HD : (h + 1) * HD].astype(F32) for h in range(heads)], axis=0
            ).astype(BF16)
            stacked[b] = q
            query_place = places(jnp.bitwise_xor(z_here, fars[b]), 0)
            begins = jnp.zeros((tokens, tokens), jnp.int32)
            edge = jnp.int32(0)
            for r in range(REQS):
                edge = edge + len_ref[group, r]
                begins = jnp.where(query_place >= edge, edge, begins)
            seen = jnp.logical_and(key_place <= query_place, key_place >= begins)
            seen = jnp.concatenate([seen.astype(F32)] * heads, axis=0)
            own = lax.dot_general(q, own_keys, NT, preferred_element_type=F32)
            own = jnp.where(seen > 0.0, own, LOW)
            highest = jnp.max(own, axis=1, keepdims=True)
            weights = jnp.exp2((own - highest) * EXP2_SCALE) * seen
            total[b] = jnp.dot(weights.astype(BF16), own_values, preferred_element_type=F32)
            top[b] = jnp.broadcast_to(highest, (rows, HD))

        def score(b, c):
            span = pl.ds(pl.multiple_of(c * wide, wide), wide)
            scores[b] = lax.dot_general(
                stacked[b], keys_ref[span, :], NT, preferred_element_type=F32
            )

        def turn(c, carry):
            span = pl.ds(pl.multiple_of(c * wide, wide), wide)
            chunk_values = jnp.concatenate(
                [values_ref[span, :], jnp.ones((wide, HD), BF16)], axis=1
            )
            for b in range(blocks):
                pieces = [
                    jnp.where(c * CHUNK + j < count, scores[b, :, j * PAGE : (j + 1) * PAGE], LOW)
                    for j in range(CHUNK)
                ]
                best = functools.reduce(jnp.maximum, pieces)
                before = top[b]
                highest = jnp.maximum(before, jnp.max(best, axis=1, keepdims=True))
                weights = jnp.concatenate(
                    [jnp.exp2((piece - highest) * EXP2_SCALE).astype(BF16) for piece in pieces],
                    axis=1,
                )
                factor = jnp.exp2((before - highest) * EXP2_SCALE)
                added = jnp.dot(weights, chunk_values, preferred_element_type=F32)
                total[b] = total[b] * jnp.concatenate([factor, factor], axis=1) + added
                top[b] = highest
                score(b, jnp.minimum(c + 1, slots // CHUNK - 1))
            return carry

        for b in range(blocks):
            score(b, 0)
        lax.fori_loop(0, turns, turn, 0)
        for b in range(blocks):
            sums = total[b, :, HD:]
            some = sums > 0.0
            safe = jnp.where(some, sums, 1.0)
            outs[b][0:rows, :] = (total[b, :, :HD] / safe).astype(BF16)
            column[0:rows, :] = jnp.where(some, top[b] * EXP2_SCALE + jnp.log2(safe), LOW)
            stats[...] = jnp.zeros((stat_rows, HD), F32)
            for part in range(parts):
                line = column[part * HD : (part + 1) * HD, :].T[0:1, :]
                for piece in range(3):
                    rounded = line.astype(BF16).astype(F32)
                    stats[3 * part + piece : 3 * part + piece + 1, :] = rounded
                    line = line - rounded
            outs[b][rows : rows + stat_rows, :] = stats[...].astype(BF16)
        if fetched:
            copy.wait()

    return pl.pallas_call(
        body,
        in_specs=[SMEM, SMEM, SMEM] + [HBM] * len(fetched) + [VMEM] * (blocks + splits + 2),
        out_specs=[VMEM] * blocks + [ANY] * len(fetched),
        out_shape=[jax.ShapeDtypeStruct((rows + stat_rows, HD), BF16)] * blocks
        + [jax.ShapeDtypeStruct((heads * HD, array.shape[1]), BF16) for array in fetched],
        scratch_shapes=[
            pltpu.VMEM((blocks, rows, HD), BF16),
            pltpu.VMEM((blocks, rows, wide), F32),
            pltpu.VMEM((blocks, rows, HD), F32),
            pltpu.VMEM((blocks, rows, 2 * HD), F32),
            pltpu.VMEM((parts * HD, HD), F32),
            pltpu.VMEM((stat_rows, HD), F32),
        ]
        + [pltpu.SemaphoreType.DMA] * len(fetched),
        compiler_params=params(40 if fetched else 16),
        cost_estimate=pl.CostEstimate(
            flops=4 * blocks * rows * slots * PAGE * HD,
            bytes_accessed=slots * PAGE * HD * 3,
            transcendentals=blocks * rows * slots * PAGE // 2,
        ),
    )(listed, lengths, place, *fetched, *queries, *suffix, keys, values)


def project(place, partials, weight, rows_each, splits, ranks, heads):
    tokens = rows_each * splits
    rows = tokens * heads
    parts = -(-rows // HD)
    width = weight.shape[1] // ranks

    def body(place_ref, *refs):
        count = len(partials)
        partial_refs, weight_ref, outs = refs[:count], refs[count], refs[count + 1 : -2]
        merged, attended = refs[-2:]
        for part in range(parts):
            length = min(HD, rows - part * HD)
            lines = []
            for ref in partial_refs:
                stat = ref[rows:, :].astype(F32)
                lines.append(
                    stat[3 * part : 3 * part + 1]
                    + stat[3 * part + 1 : 3 * part + 2]
                    + stat[3 * part + 2 : 3 * part + 3]
                )
            best = functools.reduce(jnp.maximum, lines)
            shares = [jnp.exp2(line - best) for line in lines]
            whole = functools.reduce(jnp.add, shares)
            mixed = jnp.zeros((length, HD), F32)
            for share, ref in zip(shares, partial_refs):
                factor = jnp.broadcast_to(share / whole, (HD, HD)).T[:length]
                mixed = mixed + factor * ref[part * HD : part * HD + length, :].astype(F32)
            merged[part * HD : part * HD + length, :] = mixed
        for h in range(heads):
            attended[:, h * HD : (h + 1) * HD] = merged[h * tokens : (h + 1) * tokens, :].astype(
                BF16
            )
        for rank in range(ranks):
            start = pl.multiple_of(jnp.bitwise_xor(place_ref[4], rank) * width, width)
            product = jnp.dot(
                attended[...], weight_ref[:, pl.ds(start, width)], preferred_element_type=F32
            )
            for sub in range(splits):
                out = outs[rank * splits + sub]
                out[...] = product[sub * rows_each : (sub + 1) * rows_each].astype(out.dtype)

    return pl.pallas_call(
        body,
        in_specs=[SMEM] + [VMEM] * (len(partials) + 1),
        out_specs=[VMEM] * (ranks * splits),
        out_shape=[
            jax.ShapeDtypeStruct((rows_each, width), BF16 if i else F32)
            for i in range(ranks * splits)
        ],
        scratch_shapes=[pltpu.VMEM((rows, HD), F32), pltpu.VMEM((tokens, heads * HD), BF16)],
        compiler_params=params(16),
        cost_estimate=pl.CostEstimate(
            flops=2 * tokens * weight.size, bytes_accessed=weight.size, transcendentals=0
        ),
    )(place, *partials, weight)


def local(
    hidden_in,
    kv_weight,
    queries,
    prefix_keys,
    prefix_values,
    page_table,
    suffix_lengths,
    out_weight,
):
    rows = hidden_in.shape[0]
    seq_count, ranks = lax.axis_size("seq"), lax.axis_size("tp")
    seq_rank, tp_rank = lax.axis_index("seq"), lax.axis_index("tp")
    pages = prefix_keys.shape[0]
    splits = prefix_keys.shape[2] // HD
    heads = queries.shape[1] // HD // splits
    prefix_len = pages * seq_count // GROUPS * PAGE
    blocks = seq_count // GROUPS
    depth = blocks // splits
    group = seq_rank % GROUPS
    block = seq_rank // GROUPS
    split = block % splits
    place = jnp.stack(
        [group, split, (block - split) * GROUPS * pages, block // splits, tp_rank]
    ).astype(jnp.int32)
    place = jnp.concatenate([place, page_table])

    def across(array, far=0, side=0, core=0):
        step = (far * splits + side) * GROUPS + core
        return lax.ppermute(array, "seq", [(i, i ^ step) for i in range(seq_count)])

    def columns(array, index, width):
        return lax.dynamic_slice_in_dim(array, index * width, width, 1)

    def quad(array, rank, side):
        step = side * GROUPS
        route = [
            (i * ranks + j, (i ^ step) * ranks + (j ^ rank))
            for i in range(seq_count)
            for j in range(ranks)
        ]
        return lax.ppermute(array, ("seq", "tp"), route)

    def columns(array, index, width):
        return lax.dynamic_slice_in_dim(array, index * width, width, array.ndim - 1)

    parts = [columns(queries, split, heads * HD)]
    for side in range(1, splits):
        parts.append(across(columns(queries, split ^ side, heads * HD), side=side))
    my_query = jnp.concatenate(parts, axis=0)
    far_queries = [my_query] + [across(my_query, far=far) for far in range(1, depth)]
    sent = [
        jnp.stack([columns(array, split ^ side, HD) for array in (prefix_keys, prefix_values)])
        for side in range(splits)
    ]
    arrived = [across(sent[side], side=side) for side in range(1, splits)]
    sources = [prefix_keys, prefix_values, across(sent[0], core=1)]

    *projected, listed = project_kv(
        hidden_in, kv_weight, place, ranks, pages * splits * GROUPS, my_query
    )
    others = [
        lax.ppermute(projected[rank], "tp", [(i, i ^ rank) for i in range(ranks)])
        for rank in range(1, ranks)
    ]
    late = (projected[0][0, 0] * 0).astype(jnp.int32)
    lengths = jnp.sum(
        jnp.where(jnp.arange(GROUPS)[:, None] == group, suffix_lengths + late, 0), axis=0
    )
    ends = jnp.sum(
        jnp.where(jnp.arange(REQS)[None, :] <= jnp.arange(REQS)[:, None], lengths[None, :], 0),
        axis=1,
    )
    within = block * rows + jnp.arange(rows, dtype=jnp.int32)
    begins = jnp.max(jnp.where(within[:, None] >= ends[None, :], ends[None, :], 0), axis=1)
    positions = prefix_len + within - begins
    half = HD // 2
    frequency = jnp.power(500000.0, -(jnp.arange(half, dtype=F32) * 2.0 / HD))
    angles = positions.astype(F32)[:, None] * frequency[None, :]
    cosine, sine = jnp.cos(angles), jnp.sin(angles)
    cosine = jnp.concatenate([cosine, cosine], axis=1)
    sine = jnp.concatenate([-sine, sine], axis=1)
    new_pages, *suffix = finish_kv(place, projected[0], others, cosine, sine, splits)
    suffix = suffix[:1] + [across(suffix[side], side=side) for side in range(1, splits)]

    for array in arrived:
        array = array_after(array, *others, *far_queries[1:])
        sources += [array, across(array, core=1)]
    keys, values = collect_pages(listed, place, sources, pages, splits)

    returned = []
    order = list(range(depth - 1, -1, -1))
    calls = [order[i : i + BLOCKS] for i in range(0, depth - BLOCKS, BLOCKS)]
    calls += [[far] for far in order[len(calls) * BLOCKS :]]
    for i, fars in enumerate(calls):
        sums = attend(
            listed, suffix_lengths, place, fars, [far_queries[far] for far in fars],
            suffix, keys, values, rows, None if i else out_weight,
        )
        if not i:
            weight = sums[-1]
        returned += [across(part, far=far) if far else part for far, part in zip(fars, sums)]

    products = project(place, returned, weight, rows, splits, ranks, heads)
    hidden = products[0]
    for rank in range(ranks):
        for side in range(splits):
            if rank or side:
                hidden = hidden + quad(products[rank * splits + side], rank, side).astype(F32)
    return (hidden.astype(BF16), new_pages)


def solution(mesh):
    return jax.shard_map(
        local,
        mesh=mesh,
        in_specs=(
            P("seq", "tp"),
            P("tp", None),
            P("seq", "tp"),
            P("seq", None, "tp"),
            P("seq", None, "tp"),
            P(),
            P(),
            P("tp", None),
        ),
        out_specs=(P("seq", "tp"), P("seq", "tp")),
        check_vma=False,
    )
```

```python
import functools
import math

import jax
import jax.numpy as jnp
from jax import lax
from jax.experimental import pallas as pl
from jax.experimental.pallas import tpu as pltpu
from jax.sharding import PartitionSpec as P

HD = 128
PAGE = 128
GROUPS = 2
REQS = 8
PLACE = 5
CHUNK = 4
BLOCKS = 2
AHEAD = 8
LOW = -1e30
EXP2_SCALE = math.log2(math.e) / math.sqrt(HD)
F32 = jnp.float32
BF16 = jnp.bfloat16
MIB = 1 << 20

NT = (((1,), (1,)), ((), ()))

VMEM = pl.BlockSpec(memory_space=pltpu.VMEM)
SMEM = pl.BlockSpec(memory_space=pltpu.SMEM)
ANY = pl.BlockSpec(memory_space=pl.ANY)
HBM = pl.BlockSpec(memory_space=pltpu.HBM)


TINY = pl.CostEstimate(flops=1, bytes_accessed=1, transcendentals=0)


def params(mib):
    return pltpu.CompilerParams(vmem_limit_bytes=mib * MIB)


def array_after(array, *awaited):
    def body(*refs):
        pass

    return pl.pallas_call(
        body,
        in_specs=[ANY] * (1 + len(awaited)),
        out_specs=ANY,
        out_shape=jax.ShapeDtypeStruct(array.shape, array.dtype),
        input_output_aliases={0: 0},
        compiler_params=params(2),
        cost_estimate=TINY,
    )(array, *awaited)


def project_kv(hidden_in, weight, table, ranks, slots, awaited):
    group_pages = (table.shape[0] - PLACE) // GROUPS
    rows, deep = hidden_in.shape
    width = weight.shape[1] // ranks
    steps = 8
    part = deep // steps

    def body(place_ref, hidden_ref, weight_ref, _, *refs):
        outs, (listed, buffer, sums, sem) = refs[:ranks], refs[ranks:]
        copies = [
            pltpu.make_async_copy(weight_ref.at[pl.ds(i * part, part)], buffer.at[i], sem.at[i])
            for i in range(steps)
        ]
        for copy in copies[:AHEAD]:
            copy.start()
        group, first = place_ref[0], place_ref[2]

        def look(i, number):
            slot = place_ref[PLACE + group * group_pages + i] - first
            here = jnp.logical_and(slot >= 0, slot < slots)
            listed[number + 1] = slot
            return number + here.astype(jnp.int32)

        listed[0] = lax.fori_loop(0, group_pages, look, jnp.int32(0), unroll=8)
        for i, copy in enumerate(copies):
            copy.wait()
            if i + AHEAD < steps:
                copies[i + AHEAD].start()
            product = jnp.dot(
                hidden_ref[:, i * part : (i + 1) * part],
                buffer[i],
                preferred_element_type=F32,
            )
            sums[...] = product if i == 0 else sums[...] + product
        for rank, out in enumerate(outs):
            start = pl.multiple_of(jnp.bitwise_xor(place_ref[4], rank) * width, width)
            out[...] = sums[:, pl.ds(start, width)]

    return pl.pallas_call(
        body,
        in_specs=[SMEM, VMEM, HBM, ANY],
        out_specs=[VMEM] * ranks + [SMEM],
        out_shape=[jax.ShapeDtypeStruct((rows, width), F32)] * ranks
        + [jax.ShapeDtypeStruct((slots + 2,), jnp.int32)],
        scratch_shapes=[
            pltpu.VMEM((steps, part, weight.shape[1]), BF16),
            pltpu.VMEM((rows, weight.shape[1]), F32),
            pltpu.SemaphoreType.DMA((steps,)),
        ],
        compiler_params=params(48),
        cost_estimate=TINY,
    )(table, hidden_in, weight, awaited)


def finish_kv(place, mine, others, cosine, sine, heads):
    rows = mine.shape[0]

    def body(place_ref, *refs):
        count = 1 + len(others)
        out, pieces = refs[count + 2], refs[count + 3 :]
        total = refs[0][...]
        for other in refs[1:count]:
            total = total + other[...]
        cos, sin = refs[count][...], refs[count + 1][...]
        for head in range(heads):
            key = total[:, head * 2 * HD : (head * 2 + 1) * HD]
            key = (key * cos + pltpu.roll(key, HD // 2, 1) * sin).astype(BF16)
            value = total[:, (head * 2 + 1) * HD : (head * 2 + 2) * HD].astype(BF16)
            out[:, head * 2 * HD : (head * 2 + 1) * HD] = key
            out[:, (head * 2 + 1) * HD : (head * 2 + 2) * HD] = value
            for step in range(heads):

                @pl.when(jnp.bitwise_xor(place_ref[1], step) == head)
                def _():
                    pieces[step][:, :HD] = key
                    pieces[step][:, HD:] = value

    return pl.pallas_call(
        body,
        in_specs=[SMEM] + [VMEM] * (3 + len(others)),
        out_specs=[VMEM] * (1 + heads),
        out_shape=[jax.ShapeDtypeStruct((rows, heads * 2 * HD), BF16)]
        + [jax.ShapeDtypeStruct((rows, 2 * HD), BF16)] * heads,
        compiler_params=params(4),
        cost_estimate=TINY,
    )(place, mine, *others, cosine, sine)


def collect_pages(listed, place, sources, pages, splits):
    slots = pages * splits * GROUPS

    def body(list_ref, place_ref, *refs):
        own_keys, own_values, *others = refs[: len(sources)]
        keys_out, values_out = refs[len(sources) :]
        here = place_ref[1] * GROUPS + place_ref[0]
        number = list_ref[0]

        def rows(i):
            return pl.ds(pl.multiple_of(i * PAGE, PAGE), PAGE)

        def collect(i, carry):
            slot = list_ref[1 + i]
            device = slot // pages
            page = slot - device * pages
            kind = jnp.bitwise_xor(device, here)

            @pl.when(kind == 0)
            def _():
                column = pl.ds(pl.multiple_of(place_ref[1] * HD, HD), HD)
                keys_out[rows(i), :] = own_keys[page, :, column]
                values_out[rows(i), :] = own_values[page, :, column]

            for which, other in enumerate(others):

                @pl.when(kind == which + 1)
                def _():
                    keys_out[rows(i), :] = other[0, page]
                    values_out[rows(i), :] = other[1, page]

            return carry

        lax.fori_loop(0, number, collect, 0)

        def clear(i, carry):
            values_out[rows(i), :] = jnp.zeros((PAGE, HD), BF16)
            return carry

        lax.fori_loop(number, jnp.minimum(number + CHUNK - 1, slots), clear, 0)

    return pl.pallas_call(
        body,
        in_specs=[SMEM, SMEM] + [VMEM] * len(sources),
        out_specs=[VMEM, VMEM],
        out_shape=[
            jax.ShapeDtypeStruct((slots * PAGE, HD), BF16),
            jax.ShapeDtypeStruct((slots * PAGE, HD), BF16),
        ],
        compiler_params=params(16),
        cost_estimate=TINY,
    )(listed, place, *sources)


def attend(listed, lengths, place, fars, queries, suffix, keys, values, rows_each, weight=None):
    fetched = [] if weight is None else [weight]
    tokens = queries[0].shape[0]
    splits = tokens // rows_each
    heads = queries[0].shape[1] // HD
    rows = tokens * heads
    slots = keys.shape[0] // PAGE
    wide = CHUNK * PAGE
    parts = -(-rows // HD)
    stat_rows = -(-3 * parts // 16) * 16
    blocks = len(queries)

    def body(list_ref, len_ref, place_ref, *refs):
        if fetched:
            weight_ref, rows_out, weight_sem = refs[0], refs[-8], refs[-1]
            refs = (*refs[1:-8], *refs[-7:-1])
            start = pl.multiple_of(place_ref[1] * heads * HD, heads * HD)
            copy = pltpu.make_async_copy(
                weight_ref.at[pl.ds(start, heads * HD)], rows_out, weight_sem
            )
            copy.start()
        query_refs, refs = refs[:blocks], refs[blocks:]
        suffix_refs, refs = refs[:splits], refs[splits:]
        keys_ref, values_ref, refs = refs[0], refs[1], refs[2:]
        outs, (stacked, scores, top, total, column, stats) = refs[:blocks], refs[blocks:]
        count = list_ref[0]
        turns = lax.div(count + (CHUNK - 1), CHUNK)
        group, split, z_here = place_ref[0], place_ref[1], place_ref[3]

        def places(z, axis):
            index = lax.broadcasted_iota(jnp.int32, (tokens, tokens), axis)
            result = jnp.zeros((tokens, tokens), jnp.int32)
            for sub in range(splits):
                block = z * splits + jnp.bitwise_xor(split, sub)
                result = jnp.where(
                    index >= sub * rows_each, (block - sub) * rows_each + index, result
                )
            return result

        own_kv = jnp.concatenate([ref[...].astype(F32) for ref in suffix_refs], axis=0).astype(BF16)
        own_keys = own_kv[:, :HD]
        own_values = jnp.concatenate([own_kv[:, HD:], jnp.ones((tokens, HD), BF16)], axis=1)
        key_place = places(z_here, 1)
        for b in range(blocks):
            q = jnp.concatenate(
                [query_refs[b][:, h * HD : (h + 1) * HD].astype(F32) for h in range(heads)], axis=0
            ).astype(BF16)
            stacked[b] = q
            query_place = places(jnp.bitwise_xor(z_here, fars[b]), 0)
            begins = jnp.zeros((tokens, tokens), jnp.int32)
            edge = jnp.int32(0)
            for r in range(REQS):
                edge = edge + len_ref[group, r]
                begins = jnp.where(query_place >= edge, edge, begins)
            seen = jnp.logical_and(key_place <= query_place, key_place >= begins)
            seen = jnp.concatenate([seen.astype(F32)] * heads, axis=0)
            own = lax.dot_general(q, own_keys, NT, preferred_element_type=F32)
            own = jnp.where(seen > 0.0, own, LOW)
            highest = jnp.max(own, axis=1, keepdims=True)
            weights = jnp.exp2((own - highest) * EXP2_SCALE) * seen
            total[b] = jnp.dot(weights.astype(BF16), own_values, preferred_element_type=F32)
            top[b] = jnp.broadcast_to(highest, (rows, HD))

        def score(b, c):
            span = pl.ds(pl.multiple_of(c * wide, wide), wide)
            scores[b] = lax.dot_general(
                stacked[b], keys_ref[span, :], NT, preferred_element_type=F32
            )

        def turn(c, carry):
            span = pl.ds(pl.multiple_of(c * wide, wide), wide)
            chunk_values = jnp.concatenate(
                [values_ref[span, :], jnp.ones((wide, HD), BF16)], axis=1
            )
            for b in range(blocks):
                pieces = [
                    jnp.where(c * CHUNK + j < count, scores[b, :, j * PAGE : (j + 1) * PAGE], LOW)
                    for j in range(CHUNK)
                ]
                best = functools.reduce(jnp.maximum, pieces)
                before = top[b]
                highest = jnp.maximum(before, jnp.max(best, axis=1, keepdims=True))
                weights = jnp.concatenate(
                    [jnp.exp2((piece - highest) * EXP2_SCALE).astype(BF16) for piece in pieces],
                    axis=1,
                )
                factor = jnp.exp2((before - highest) * EXP2_SCALE)
                added = jnp.dot(weights, chunk_values, preferred_element_type=F32)
                total[b] = total[b] * jnp.concatenate([factor, factor], axis=1) + added
                top[b] = highest
                score(b, jnp.minimum(c + 1, slots // CHUNK - 1))
            return carry

        for b in range(blocks):
            score(b, 0)
        lax.fori_loop(0, turns, turn, 0)
        for b in range(blocks):
            sums = total[b, :, HD:]
            some = sums > 0.0
            safe = jnp.where(some, sums, 1.0)
            outs[b][0:rows, :] = (total[b, :, :HD] / safe).astype(BF16)
            column[0:rows, :] = jnp.where(some, top[b] * EXP2_SCALE + jnp.log2(safe), LOW)
            stats[...] = jnp.zeros((stat_rows, HD), F32)
            for part in range(parts):
                line = column[part * HD : (part + 1) * HD, :].T[0:1, :]
                for piece in range(3):
                    rounded = line.astype(BF16).astype(F32)
                    stats[3 * part + piece : 3 * part + piece + 1, :] = rounded
                    line = line - rounded
            outs[b][rows : rows + stat_rows, :] = stats[...].astype(BF16)
        if fetched:
            copy.wait()

    return pl.pallas_call(
        body,
        in_specs=[SMEM, SMEM, SMEM] + [HBM] * len(fetched) + [VMEM] * (blocks + splits + 2),
        out_specs=[VMEM] * blocks + [ANY] * len(fetched),
        out_shape=[jax.ShapeDtypeStruct((rows + stat_rows, HD), BF16)] * blocks
        + [jax.ShapeDtypeStruct((heads * HD, array.shape[1]), BF16) for array in fetched],
        scratch_shapes=[
            pltpu.VMEM((blocks, rows, HD), BF16),
            pltpu.VMEM((blocks, rows, wide), F32),
            pltpu.VMEM((blocks, rows, HD), F32),
            pltpu.VMEM((blocks, rows, 2 * HD), F32),
            pltpu.VMEM((parts * HD, HD), F32),
            pltpu.VMEM((stat_rows, HD), F32),
        ]
        + [pltpu.SemaphoreType.DMA] * len(fetched),
        compiler_params=params(40 if fetched else 16),
        cost_estimate=pl.CostEstimate(
            flops=4 * blocks * rows * slots * PAGE * HD,
            bytes_accessed=slots * PAGE * HD * 3,
            transcendentals=blocks * rows * slots * PAGE // 2,
        ),
    )(listed, lengths, place, *fetched, *queries, *suffix, keys, values)


def project(place, partials, weight, rows_each, splits, ranks, heads):
    tokens = rows_each * splits
    rows = tokens * heads
    parts = -(-rows // HD)
    width = weight.shape[1] // ranks

    def body(place_ref, *refs):
        count = len(partials)
        partial_refs, weight_ref, outs = refs[:count], refs[count], refs[count + 1 : -2]
        merged, attended = refs[-2:]
        for part in range(parts):
            length = min(HD, rows - part * HD)
            lines = []
            for ref in partial_refs:
                stat = ref[rows:, :].astype(F32)
                lines.append(
                    stat[3 * part : 3 * part + 1]
                    + stat[3 * part + 1 : 3 * part + 2]
                    + stat[3 * part + 2 : 3 * part + 3]
                )
            best = functools.reduce(jnp.maximum, lines)
            shares = [jnp.exp2(line - best) for line in lines]
            whole = functools.reduce(jnp.add, shares)
            mixed = jnp.zeros((length, HD), F32)
            for share, ref in zip(shares, partial_refs):
                factor = jnp.broadcast_to(share / whole, (HD, HD)).T[:length]
                mixed = mixed + factor * ref[part * HD : part * HD + length, :].astype(F32)
            merged[part * HD : part * HD + length, :] = mixed
        for h in range(heads):
            attended[:, h * HD : (h + 1) * HD] = merged[h * tokens : (h + 1) * tokens, :].astype(
                BF16
            )
        for rank in range(ranks):
            start = pl.multiple_of(jnp.bitwise_xor(place_ref[4], rank) * width, width)
            product = jnp.dot(
                attended[...], weight_ref[:, pl.ds(start, width)], preferred_element_type=F32
            )
            for sub in range(splits):
                out = outs[rank * splits + sub]
                out[...] = product[sub * rows_each : (sub + 1) * rows_each].astype(out.dtype)

    return pl.pallas_call(
        body,
        in_specs=[SMEM] + [VMEM] * (len(partials) + 1),
        out_specs=[VMEM] * (ranks * splits),
        out_shape=[
            jax.ShapeDtypeStruct((rows_each, width), BF16 if i else F32)
            for i in range(ranks * splits)
        ],
        scratch_shapes=[pltpu.VMEM((rows, HD), F32), pltpu.VMEM((tokens, heads * HD), BF16)],
        compiler_params=params(16),
        cost_estimate=pl.CostEstimate(
            flops=2 * tokens * weight.size, bytes_accessed=weight.size, transcendentals=0
        ),
    )(place, *partials, weight)


def local(
    hidden_in,
    kv_weight,
    queries,
    prefix_keys,
    prefix_values,
    page_table,
    suffix_lengths,
    out_weight,
):
    rows = hidden_in.shape[0]
    seq_count, ranks = lax.axis_size("seq"), lax.axis_size("tp")
    seq_rank, tp_rank = lax.axis_index("seq"), lax.axis_index("tp")
    pages = prefix_keys.shape[0]
    splits = prefix_keys.shape[2] // HD
    heads = queries.shape[1] // HD // splits
    prefix_len = pages * seq_count // GROUPS * PAGE
    blocks = seq_count // GROUPS
    depth = blocks // splits
    group = seq_rank % GROUPS
    block = seq_rank // GROUPS
    split = block % splits
    place = jnp.stack(
        [group, split, (block - split) * GROUPS * pages, block // splits, tp_rank]
    ).astype(jnp.int32)
    place = jnp.concatenate([place, page_table])

    def across(array, far=0, side=0, core=0):
        step = (far * splits + side) * GROUPS + core
        return lax.ppermute(array, "seq", [(i, i ^ step) for i in range(seq_count)])

    def columns(array, index, width):
        return lax.dynamic_slice_in_dim(array, index * width, width, 1)

    def quad(array, rank, side):
        step = side * GROUPS
        route = [
            (i * ranks + j, (i ^ step) * ranks + (j ^ rank))
            for i in range(seq_count)
            for j in range(ranks)
        ]
        return lax.ppermute(array, ("seq", "tp"), route)

    def columns(array, index, width):
        return lax.dynamic_slice_in_dim(array, index * width, width, array.ndim - 1)

    parts = [columns(queries, split, heads * HD)]
    for side in range(1, splits):
        parts.append(across(columns(queries, split ^ side, heads * HD), side=side))
    my_query = jnp.concatenate(parts, axis=0)
    far_queries = [my_query] + [across(my_query, far=far) for far in range(1, depth)]
    sent = [
        jnp.stack([columns(array, split ^ side, HD) for array in (prefix_keys, prefix_values)])
        for side in range(splits)
    ]
    arrived = [across(sent[side], side=side) for side in range(1, splits)]
    sources = [prefix_keys, prefix_values, across(sent[0], core=1)]

    *projected, listed = project_kv(
        hidden_in, kv_weight, place, ranks, pages * splits * GROUPS, my_query
    )
    others = [
        lax.ppermute(projected[rank], "tp", [(i, i ^ rank) for i in range(ranks)])
        for rank in range(1, ranks)
    ]
    late = (far_queries[-1][0, 0] * 0).astype(jnp.int32)
    lengths = jnp.sum(
        jnp.where(jnp.arange(GROUPS)[:, None] == group, suffix_lengths + late, 0), axis=0
    )
    ends = jnp.sum(
        jnp.where(jnp.arange(REQS)[None, :] <= jnp.arange(REQS)[:, None], lengths[None, :], 0),
        axis=1,
    )
    within = block * rows + jnp.arange(rows, dtype=jnp.int32)
    begins = jnp.max(jnp.where(within[:, None] >= ends[None, :], ends[None, :], 0), axis=1)
    positions = prefix_len + within - begins
    half = HD // 2
    frequency = jnp.power(500000.0, -(jnp.arange(half, dtype=F32) * 2.0 / HD))
    angles = positions.astype(F32)[:, None] * frequency[None, :]
    cosine, sine = jnp.cos(angles), jnp.sin(angles)
    cosine = jnp.concatenate([cosine, cosine], axis=1)
    sine = jnp.concatenate([-sine, sine], axis=1)
    new_pages, *suffix = finish_kv(place, projected[0], others, cosine, sine, splits)
    suffix = suffix[:1] + [across(suffix[side], side=side) for side in range(1, splits)]

    for array in arrived:
        array = array_after(array, projected[0], *far_queries[1:])
        sources += [array, across(array, core=1)]
    keys, values = collect_pages(listed, place, sources, pages, splits)

    returned = []
    order = list(range(depth - 1, -1, -1))
    calls = [order[i : i + BLOCKS] for i in range(0, depth - BLOCKS, BLOCKS)]
    calls += [[far] for far in order[len(calls) * BLOCKS :]]
    for i, fars in enumerate(calls):
        sums = attend(
            listed, suffix_lengths, place, fars, [far_queries[far] for far in fars],
            suffix, keys, values, rows, None if i else out_weight,
        )
        if not i:
            weight = sums[-1]
        returned += [across(part, far=far) if far else part for far, part in zip(fars, sums)]

    products = project(place, returned, weight, rows, splits, ranks, heads)
    hidden = products[0]
    for rank in range(ranks):
        for side in range(splits):
            if rank or side:
                hidden = hidden + quad(products[rank * splits + side], rank, side).astype(F32)
    return (hidden.astype(BF16), new_pages)


def solution(mesh):
    return jax.shard_map(
        local,
        mesh=mesh,
        in_specs=(
            P("seq", "tp"),
            P("tp", None),
            P("seq", "tp"),
            P("seq", None, "tp"),
            P("seq", None, "tp"),
            P(),
            P(),
            P("tp", None),
        ),
        out_specs=(P("seq", "tp"), P("seq", "tp")),
        check_vma=False,
    )
```

```python
import functools
import math

import jax
import jax.numpy as jnp
from jax import lax
from jax.experimental import pallas as pl
from jax.experimental.pallas import tpu as pltpu
from jax.sharding import PartitionSpec as P

HD = 128
PAGE = 128
GROUPS = 2
REQS = 8
PLACE = 5
CHUNK = 4
BLOCKS = 2
AHEAD = 8
LOW = -1e30
EXP2_SCALE = math.log2(math.e) / math.sqrt(HD)
F32 = jnp.float32
BF16 = jnp.bfloat16
MIB = 1 << 20

NT = (((1,), (1,)), ((), ()))

VMEM = pl.BlockSpec(memory_space=pltpu.VMEM)
SMEM = pl.BlockSpec(memory_space=pltpu.SMEM)
ANY = pl.BlockSpec(memory_space=pl.ANY)
HBM = pl.BlockSpec(memory_space=pltpu.HBM)


TINY = pl.CostEstimate(flops=1, bytes_accessed=1, transcendentals=0)


def params(mib):
    return pltpu.CompilerParams(vmem_limit_bytes=mib * MIB)


def array_after(array, *awaited):
    def body(*refs):
        pass

    return pl.pallas_call(
        body,
        in_specs=[ANY] * (1 + len(awaited)),
        out_specs=ANY,
        out_shape=jax.ShapeDtypeStruct(array.shape, array.dtype),
        input_output_aliases={0: 0},
        compiler_params=params(2),
        cost_estimate=TINY,
    )(array, *awaited)


def project_kv(hidden_in, weight, table, ranks, slots, awaited):
    group_pages = (table.shape[0] - PLACE) // GROUPS
    rows, deep = hidden_in.shape
    width = weight.shape[1] // ranks
    steps = 8
    part = deep // steps

    def body(place_ref, hidden_ref, weight_ref, _, *refs):
        outs, (listed, buffer, sums, sem) = refs[:ranks], refs[ranks:]
        copies = [
            pltpu.make_async_copy(weight_ref.at[pl.ds(i * part, part)], buffer.at[i], sem.at[i])
            for i in range(steps)
        ]
        for copy in copies[:AHEAD]:
            copy.start()
        group, first = place_ref[0], place_ref[2]

        def look(i, number):
            slot = place_ref[PLACE + group * group_pages + i] - first
            here = jnp.logical_and(slot >= 0, slot < slots)
            listed[number + 1] = slot
            return number + here.astype(jnp.int32)

        listed[0] = lax.fori_loop(0, group_pages, look, jnp.int32(0), unroll=8)
        for i, copy in enumerate(copies):
            copy.wait()
            if i + AHEAD < steps:
                copies[i + AHEAD].start()
            product = jnp.dot(
                hidden_ref[:, i * part : (i + 1) * part],
                buffer[i],
                preferred_element_type=F32,
            )
            sums[...] = product if i == 0 else sums[...] + product
        for rank, out in enumerate(outs):
            start = pl.multiple_of(jnp.bitwise_xor(place_ref[4], rank) * width, width)
            out[...] = sums[:, pl.ds(start, width)]

    return pl.pallas_call(
        body,
        in_specs=[SMEM, VMEM, HBM, ANY],
        out_specs=[VMEM] * ranks + [SMEM],
        out_shape=[jax.ShapeDtypeStruct((rows, width), F32)] * ranks
        + [jax.ShapeDtypeStruct((slots + 2,), jnp.int32)],
        scratch_shapes=[
            pltpu.VMEM((steps, part, weight.shape[1]), BF16),
            pltpu.VMEM((rows, weight.shape[1]), F32),
            pltpu.SemaphoreType.DMA((steps,)),
        ],
        compiler_params=params(48),
        cost_estimate=TINY,
    )(table, hidden_in, weight, awaited)


def finish_kv(place, mine, others, cosine, sine, heads):
    rows = mine.shape[0]

    def body(place_ref, *refs):
        count = 1 + len(others)
        out, pieces = refs[count + 2], refs[count + 3 :]
        total = refs[0][...]
        for other in refs[1:count]:
            total = total + other[...]
        cos, sin = refs[count][...], refs[count + 1][...]
        for head in range(heads):
            key = total[:, head * 2 * HD : (head * 2 + 1) * HD]
            key = (key * cos + pltpu.roll(key, HD // 2, 1) * sin).astype(BF16)
            value = total[:, (head * 2 + 1) * HD : (head * 2 + 2) * HD].astype(BF16)
            out[:, head * 2 * HD : (head * 2 + 1) * HD] = key
            out[:, (head * 2 + 1) * HD : (head * 2 + 2) * HD] = value
            for step in range(heads):

                @pl.when(jnp.bitwise_xor(place_ref[1], step) == head)
                def _():
                    pieces[step][:, :HD] = key
                    pieces[step][:, HD:] = value

    return pl.pallas_call(
        body,
        in_specs=[SMEM] + [VMEM] * (3 + len(others)),
        out_specs=[VMEM] * (1 + heads),
        out_shape=[jax.ShapeDtypeStruct((rows, heads * 2 * HD), BF16)]
        + [jax.ShapeDtypeStruct((rows, 2 * HD), BF16)] * heads,
        compiler_params=params(4),
        cost_estimate=TINY,
    )(place, mine, *others, cosine, sine)


def collect_pages(listed, place, sources, pages, splits):
    slots = pages * splits * GROUPS

    def body(list_ref, place_ref, *refs):
        own_keys, own_values, *others = refs[: len(sources)]
        keys_out, values_out = refs[len(sources) :]
        here = place_ref[1] * GROUPS + place_ref[0]
        number = list_ref[0]

        def rows(i):
            return pl.ds(pl.multiple_of(i * PAGE, PAGE), PAGE)

        def collect(i, carry):
            slot = list_ref[1 + i]
            device = slot // pages
            page = slot - device * pages
            kind = jnp.bitwise_xor(device, here)

            @pl.when(kind == 0)
            def _():
                column = pl.ds(pl.multiple_of(place_ref[1] * HD, HD), HD)
                keys_out[rows(i), :] = own_keys[page, :, column]
                values_out[rows(i), :] = own_values[page, :, column]

            for which, other in enumerate(others):

                @pl.when(kind == which + 1)
                def _():
                    keys_out[rows(i), :] = other[0, page]
                    values_out[rows(i), :] = other[1, page]

            return carry

        lax.fori_loop(0, number, collect, 0)

        def clear(i, carry):
            values_out[rows(i), :] = jnp.zeros((PAGE, HD), BF16)
            return carry

        lax.fori_loop(number, jnp.minimum(number + CHUNK - 1, slots), clear, 0)

    return pl.pallas_call(
        body,
        in_specs=[SMEM, SMEM] + [VMEM] * len(sources),
        out_specs=[VMEM, VMEM],
        out_shape=[
            jax.ShapeDtypeStruct((slots * PAGE, HD), BF16),
            jax.ShapeDtypeStruct((slots * PAGE, HD), BF16),
        ],
        compiler_params=params(16),
        cost_estimate=TINY,
    )(listed, place, *sources)


def attend(listed, lengths, place, fars, queries, suffix, keys, values, rows_each, weight=None):
    fetched = [] if weight is None else [weight]
    tokens = queries[0].shape[0]
    splits = tokens // rows_each
    heads = queries[0].shape[1] // HD
    rows = tokens * heads
    slots = keys.shape[0] // PAGE
    wide = CHUNK * PAGE
    parts = -(-rows // HD)
    stat_rows = -(-3 * parts // 16) * 16
    blocks = len(queries)

    def body(list_ref, len_ref, place_ref, *refs):
        if fetched:
            weight_ref, rows_out, weight_sem = refs[0], refs[-8], refs[-1]
            refs = (*refs[1:-8], *refs[-7:-1])
            start = pl.multiple_of(place_ref[1] * heads * HD, heads * HD)
            copy = pltpu.make_async_copy(
                weight_ref.at[pl.ds(start, heads * HD)], rows_out, weight_sem
            )
            copy.start()
        query_refs, refs = refs[:blocks], refs[blocks:]
        suffix_refs, refs = refs[:splits], refs[splits:]
        keys_ref, values_ref, refs = refs[0], refs[1], refs[2:]
        outs, (stacked, scores, top, total, column, stats) = refs[:blocks], refs[blocks:]
        count = list_ref[0]
        turns = lax.div(count + (CHUNK - 1), CHUNK)
        group, split, z_here = place_ref[0], place_ref[1], place_ref[3]

        def places(z, axis):
            index = lax.broadcasted_iota(jnp.int32, (tokens, tokens), axis)
            result = jnp.zeros((tokens, tokens), jnp.int32)
            for sub in range(splits):
                block = z * splits + jnp.bitwise_xor(split, sub)
                result = jnp.where(
                    index >= sub * rows_each, (block - sub) * rows_each + index, result
                )
            return result

        own_kv = jnp.concatenate([ref[...].astype(F32) for ref in suffix_refs], axis=0).astype(BF16)
        own_keys = own_kv[:, :HD]
        own_values = jnp.concatenate([own_kv[:, HD:], jnp.ones((tokens, HD), BF16)], axis=1)
        key_place = places(z_here, 1)
        for b in range(blocks):
            q = jnp.concatenate(
                [query_refs[b][:, h * HD : (h + 1) * HD].astype(F32) for h in range(heads)], axis=0
            ).astype(BF16)
            stacked[b] = q
            query_place = places(jnp.bitwise_xor(z_here, fars[b]), 0)
            begins = jnp.zeros((tokens, tokens), jnp.int32)
            edge = jnp.int32(0)
            for r in range(REQS):
                edge = edge + len_ref[group, r]
                begins = jnp.where(query_place >= edge, edge, begins)
            seen = jnp.logical_and(key_place <= query_place, key_place >= begins)
            seen = jnp.concatenate([seen.astype(F32)] * heads, axis=0)
            own = lax.dot_general(q, own_keys, NT, preferred_element_type=F32)
            own = jnp.where(seen > 0.0, own, LOW)
            highest = jnp.max(own, axis=1, keepdims=True)
            weights = jnp.exp2((own - highest) * EXP2_SCALE) * seen
            total[b] = jnp.dot(weights.astype(BF16), own_values, preferred_element_type=F32)
            top[b] = jnp.broadcast_to(highest, (rows, HD))

        def score(b, c):
            span = pl.ds(pl.multiple_of(c * wide, wide), wide)
            scores[b] = lax.dot_general(
                stacked[b], keys_ref[span, :], NT, preferred_element_type=F32
            )

        def turn(c, last):
            span = pl.ds(pl.multiple_of(c * wide, wide), wide)
            chunk_values = jnp.concatenate(
                [values_ref[span, :], jnp.ones((wide, HD), BF16)], axis=1
            )
            for b in range(blocks):
                pieces = [scores[b, :, j * PAGE : (j + 1) * PAGE] for j in range(CHUNK)]
                if last:
                    pieces = [
                        jnp.where(c * CHUNK + j < count, piece, LOW)
                        for j, piece in enumerate(pieces)
                    ]
                best = functools.reduce(jnp.maximum, pieces)
                before = top[b]
                highest = jnp.maximum(before, jnp.max(best, axis=1, keepdims=True))
                weights = jnp.concatenate(
                    [jnp.exp2((piece - highest) * EXP2_SCALE).astype(BF16) for piece in pieces],
                    axis=1,
                )
                factor = jnp.exp2((before - highest) * EXP2_SCALE)
                added = jnp.dot(weights, chunk_values, preferred_element_type=F32)
                total[b] = total[b] * jnp.concatenate([factor, factor], axis=1) + added
                top[b] = highest
                if not last:
                    score(b, c + 1)

        def full_turn(c, carry):
            turn(c, False)
            return carry

        for b in range(blocks):
            score(b, 0)
        lax.fori_loop(0, turns - 1, full_turn, 0)

        @pl.when(turns > 0)
        def _():
            turn(turns - 1, True)

        for b in range(blocks):
            sums = total[b, :, HD:]
            some = sums > 0.0
            safe = jnp.where(some, sums, 1.0)
            outs[b][0:rows, :] = (total[b, :, :HD] / safe).astype(BF16)
            column[0:rows, :] = jnp.where(some, top[b] * EXP2_SCALE + jnp.log2(safe), LOW)
            stats[...] = jnp.zeros((stat_rows, HD), F32)
            for part in range(parts):
                line = column[part * HD : (part + 1) * HD, :].T[0:1, :]
                for piece in range(3):
                    rounded = line.astype(BF16).astype(F32)
                    stats[3 * part + piece : 3 * part + piece + 1, :] = rounded
                    line = line - rounded
            outs[b][rows : rows + stat_rows, :] = stats[...].astype(BF16)
        if fetched:
            copy.wait()

    return pl.pallas_call(
        body,
        in_specs=[SMEM, SMEM, SMEM] + [HBM] * len(fetched) + [VMEM] * (blocks + splits + 2),
        out_specs=[VMEM] * blocks + [ANY] * len(fetched),
        out_shape=[jax.ShapeDtypeStruct((rows + stat_rows, HD), BF16)] * blocks
        + [jax.ShapeDtypeStruct((heads * HD, array.shape[1]), BF16) for array in fetched],
        scratch_shapes=[
            pltpu.VMEM((blocks, rows, HD), BF16),
            pltpu.VMEM((blocks, rows, wide), F32),
            pltpu.VMEM((blocks, rows, HD), F32),
            pltpu.VMEM((blocks, rows, 2 * HD), F32),
            pltpu.VMEM((parts * HD, HD), F32),
            pltpu.VMEM((stat_rows, HD), F32),
        ]
        + [pltpu.SemaphoreType.DMA] * len(fetched),
        compiler_params=params(40 if fetched else 16),
        cost_estimate=pl.CostEstimate(
            flops=4 * blocks * rows * slots * PAGE * HD,
            bytes_accessed=slots * PAGE * HD * 3,
            transcendentals=blocks * rows * slots * PAGE // 2,
        ),
    )(listed, lengths, place, *fetched, *queries, *suffix, keys, values)


def project(place, partials, weight, rows_each, splits, ranks, heads):
    tokens = rows_each * splits
    rows = tokens * heads
    parts = -(-rows // HD)
    width = weight.shape[1] // ranks

    def body(place_ref, *refs):
        count = len(partials)
        partial_refs, weight_ref, outs = refs[:count], refs[count], refs[count + 1 : -2]
        merged, attended = refs[-2:]
        for part in range(parts):
            length = min(HD, rows - part * HD)
            lines = []
            for ref in partial_refs:
                stat = ref[rows:, :].astype(F32)
                lines.append(
                    stat[3 * part : 3 * part + 1]
                    + stat[3 * part + 1 : 3 * part + 2]
                    + stat[3 * part + 2 : 3 * part + 3]
                )
            best = functools.reduce(jnp.maximum, lines)
            shares = [jnp.exp2(line - best) for line in lines]
            whole = functools.reduce(jnp.add, shares)
            mixed = jnp.zeros((length, HD), F32)
            for share, ref in zip(shares, partial_refs):
                factor = jnp.broadcast_to(share / whole, (HD, HD)).T[:length]
                mixed = mixed + factor * ref[part * HD : part * HD + length, :].astype(F32)
            merged[part * HD : part * HD + length, :] = mixed
        for h in range(heads):
            attended[:, h * HD : (h + 1) * HD] = merged[h * tokens : (h + 1) * tokens, :].astype(
                BF16
            )
        for rank in range(ranks):
            start = pl.multiple_of(jnp.bitwise_xor(place_ref[4], rank) * width, width)
            product = jnp.dot(
                attended[...], weight_ref[:, pl.ds(start, width)], preferred_element_type=F32
            )
            for sub in range(splits):
                out = outs[rank * splits + sub]
                out[...] = product[sub * rows_each : (sub + 1) * rows_each].astype(out.dtype)

    return pl.pallas_call(
        body,
        in_specs=[SMEM] + [VMEM] * (len(partials) + 1),
        out_specs=[VMEM] * (ranks * splits),
        out_shape=[
            jax.ShapeDtypeStruct((rows_each, width), BF16 if i else F32)
            for i in range(ranks * splits)
        ],
        scratch_shapes=[pltpu.VMEM((rows, HD), F32), pltpu.VMEM((tokens, heads * HD), BF16)],
        compiler_params=params(16),
        cost_estimate=pl.CostEstimate(
            flops=2 * tokens * weight.size, bytes_accessed=weight.size, transcendentals=0
        ),
    )(place, *partials, weight)


def local(
    hidden_in,
    kv_weight,
    queries,
    prefix_keys,
    prefix_values,
    page_table,
    suffix_lengths,
    out_weight,
):
    rows = hidden_in.shape[0]
    seq_count, ranks = lax.axis_size("seq"), lax.axis_size("tp")
    seq_rank, tp_rank = lax.axis_index("seq"), lax.axis_index("tp")
    pages = prefix_keys.shape[0]
    splits = prefix_keys.shape[2] // HD
    heads = queries.shape[1] // HD // splits
    prefix_len = pages * seq_count // GROUPS * PAGE
    blocks = seq_count // GROUPS
    depth = blocks // splits
    group = seq_rank % GROUPS
    block = seq_rank // GROUPS
    split = block % splits
    place = jnp.stack(
        [group, split, (block - split) * GROUPS * pages, block // splits, tp_rank]
    ).astype(jnp.int32)
    place = jnp.concatenate([place, page_table])

    def across(array, far=0, side=0, core=0):
        step = (far * splits + side) * GROUPS + core
        return lax.ppermute(array, "seq", [(i, i ^ step) for i in range(seq_count)])

    def columns(array, index, width):
        return lax.dynamic_slice_in_dim(array, index * width, width, 1)

    def quad(array, rank, side):
        step = side * GROUPS
        route = [
            (i * ranks + j, (i ^ step) * ranks + (j ^ rank))
            for i in range(seq_count)
            for j in range(ranks)
        ]
        return lax.ppermute(array, ("seq", "tp"), route)

    def columns(array, index, width):
        return lax.dynamic_slice_in_dim(array, index * width, width, array.ndim - 1)

    parts = [columns(queries, split, heads * HD)]
    for side in range(1, splits):
        parts.append(across(columns(queries, split ^ side, heads * HD), side=side))
    my_query = jnp.concatenate(parts, axis=0)
    far_queries = [my_query] + [across(my_query, far=far) for far in range(1, depth)]
    sent = [
        jnp.stack([columns(array, split ^ side, HD) for array in (prefix_keys, prefix_values)])
        for side in range(splits)
    ]
    arrived = [across(sent[side], side=side) for side in range(1, splits)]
    sources = [prefix_keys, prefix_values, across(sent[0], core=1)]

    *projected, listed = project_kv(
        hidden_in, kv_weight, place, ranks, pages * splits * GROUPS, my_query
    )
    others = [
        lax.ppermute(projected[rank], "tp", [(i, i ^ rank) for i in range(ranks)])
        for rank in range(1, ranks)
    ]
    late = (projected[0][0, 0] * 0).astype(jnp.int32)
    lengths = jnp.sum(
        jnp.where(jnp.arange(GROUPS)[:, None] == group, suffix_lengths + late, 0), axis=0
    )
    ends = jnp.sum(
        jnp.where(jnp.arange(REQS)[None, :] <= jnp.arange(REQS)[:, None], lengths[None, :], 0),
        axis=1,
    )
    within = block * rows + jnp.arange(rows, dtype=jnp.int32)
    begins = jnp.max(jnp.where(within[:, None] >= ends[None, :], ends[None, :], 0), axis=1)
    positions = prefix_len + within - begins
    half = HD // 2
    frequency = jnp.power(500000.0, -(jnp.arange(half, dtype=F32) * 2.0 / HD))
    angles = positions.astype(F32)[:, None] * frequency[None, :]
    cosine, sine = jnp.cos(angles), jnp.sin(angles)
    cosine = jnp.concatenate([cosine, cosine], axis=1)
    sine = jnp.concatenate([-sine, sine], axis=1)
    new_pages, *suffix = finish_kv(place, projected[0], others, cosine, sine, splits)
    suffix = suffix[:1] + [across(suffix[side], side=side) for side in range(1, splits)]

    for array in arrived:
        array = array_after(array, *others, *far_queries[1:])
        sources += [array, across(array, core=1)]
    keys, values = collect_pages(listed, place, sources, pages, splits)

    returned = []
    order = list(range(depth - 1, -1, -1))
    calls = [order[i : i + BLOCKS] for i in range(0, depth - BLOCKS, BLOCKS)]
    calls += [[far] for far in order[len(calls) * BLOCKS :]]
    for i, fars in enumerate(calls):
        sums = attend(
            listed, suffix_lengths, place, fars, [far_queries[far] for far in fars],
            suffix, keys, values, rows, None if i else out_weight,
        )
        if not i:
            weight = sums[-1]
        returned += [across(part, far=far) if far else part for far, part in zip(fars, sums)]

    products = project(place, returned, weight, rows, splits, ranks, heads)
    hidden = products[0]
    for rank in range(ranks):
        for side in range(splits):
            if rank or side:
                hidden = hidden + quad(products[rank * splits + side], rank, side).astype(F32)
    return (hidden.astype(BF16), new_pages)


def solution(mesh):
    return jax.shard_map(
        local,
        mesh=mesh,
        in_specs=(
            P("seq", "tp"),
            P("tp", None),
            P("seq", "tp"),
            P("seq", None, "tp"),
            P("seq", None, "tp"),
            P(),
            P(),
            P("tp", None),
        ),
        out_specs=(P("seq", "tp"), P("seq", "tp")),
        check_vma=False,
    )
```

```python
import functools
import math

import jax
import jax.numpy as jnp
from jax import lax
from jax.experimental import pallas as pl
from jax.experimental.pallas import tpu as pltpu
from jax.sharding import PartitionSpec as P

HD = 128
PAGE = 128
GROUPS = 2
REQS = 8
PLACE = 5
CHUNK = 4
BLOCKS = 2
AHEAD = 8
LOW = -1e30
EXP2_SCALE = math.log2(math.e) / math.sqrt(HD)
F32 = jnp.float32
BF16 = jnp.bfloat16
MIB = 1 << 20

NT = (((1,), (1,)), ((), ()))

VMEM = pl.BlockSpec(memory_space=pltpu.VMEM)
SMEM = pl.BlockSpec(memory_space=pltpu.SMEM)
ANY = pl.BlockSpec(memory_space=pl.ANY)
HBM = pl.BlockSpec(memory_space=pltpu.HBM)


TINY = pl.CostEstimate(flops=1, bytes_accessed=1, transcendentals=0)


def params(mib):
    return pltpu.CompilerParams(vmem_limit_bytes=mib * MIB)


def array_after(array, *awaited):
    def body(*refs):
        pass

    return pl.pallas_call(
        body,
        in_specs=[ANY] * (1 + len(awaited)),
        out_specs=ANY,
        out_shape=jax.ShapeDtypeStruct(array.shape, array.dtype),
        input_output_aliases={0: 0},
        compiler_params=params(2),
        cost_estimate=TINY,
    )(array, *awaited)


def project_kv(hidden_in, weight, table, ranks, slots, awaited):
    group_pages = (table.shape[0] - PLACE) // GROUPS
    rows, deep = hidden_in.shape
    width = weight.shape[1] // ranks
    steps = 8
    part = deep // steps

    def body(place_ref, hidden_ref, weight_ref, _, *refs):
        outs, (listed, buffer, sums, sem) = refs[:ranks], refs[ranks:]
        copies = [
            pltpu.make_async_copy(weight_ref.at[pl.ds(i * part, part)], buffer.at[i], sem.at[i])
            for i in range(steps)
        ]
        for copy in copies[:AHEAD]:
            copy.start()
        group, first = place_ref[0], place_ref[2]

        def look(i, number):
            slot = place_ref[PLACE + group * group_pages + i] - first
            here = jnp.logical_and(slot >= 0, slot < slots)
            listed[number + 1] = slot
            return number + here.astype(jnp.int32)

        listed[0] = lax.fori_loop(0, group_pages, look, jnp.int32(0), unroll=8)
        for i, copy in enumerate(copies):
            copy.wait()
            if i + AHEAD < steps:
                copies[i + AHEAD].start()
            product = jnp.dot(
                hidden_ref[:, i * part : (i + 1) * part],
                buffer[i],
                preferred_element_type=F32,
            )
            sums[...] = product if i == 0 else sums[...] + product
        for rank, out in enumerate(outs):
            start = pl.multiple_of(jnp.bitwise_xor(place_ref[4], rank) * width, width)
            out[...] = sums[:, pl.ds(start, width)]

    return pl.pallas_call(
        body,
        in_specs=[SMEM, VMEM, HBM, ANY],
        out_specs=[VMEM] * ranks + [SMEM],
        out_shape=[jax.ShapeDtypeStruct((rows, width), F32)] * ranks
        + [jax.ShapeDtypeStruct((slots + 2,), jnp.int32)],
        scratch_shapes=[
            pltpu.VMEM((steps, part, weight.shape[1]), BF16),
            pltpu.VMEM((rows, weight.shape[1]), F32),
            pltpu.SemaphoreType.DMA((steps,)),
        ],
        compiler_params=params(48),
        cost_estimate=TINY,
    )(table, hidden_in, weight, awaited)


def finish_kv(place, mine, others, cosine, sine, heads):
    rows = mine.shape[0]

    def body(place_ref, *refs):
        count = 1 + len(others)
        out, pieces = refs[count + 2], refs[count + 3 :]
        total = refs[0][...]
        for other in refs[1:count]:
            total = total + other[...]
        cos, sin = refs[count][...], refs[count + 1][...]
        for head in range(heads):
            key = total[:, head * 2 * HD : (head * 2 + 1) * HD]
            key = (key * cos + pltpu.roll(key, HD // 2, 1) * sin).astype(BF16)
            value = total[:, (head * 2 + 1) * HD : (head * 2 + 2) * HD].astype(BF16)
            out[:, head * 2 * HD : (head * 2 + 1) * HD] = key
            out[:, (head * 2 + 1) * HD : (head * 2 + 2) * HD] = value
            for step in range(heads):

                @pl.when(jnp.bitwise_xor(place_ref[1], step) == head)
                def _():
                    pieces[step][:, :HD] = key
                    pieces[step][:, HD:] = value

    return pl.pallas_call(
        body,
        in_specs=[SMEM] + [VMEM] * (3 + len(others)),
        out_specs=[VMEM] * (1 + heads),
        out_shape=[jax.ShapeDtypeStruct((rows, heads * 2 * HD), BF16)]
        + [jax.ShapeDtypeStruct((rows, 2 * HD), BF16)] * heads,
        compiler_params=params(4),
        cost_estimate=TINY,
    )(place, mine, *others, cosine, sine)


def collect_pages(listed, place, sources, pages, splits):
    slots = pages * splits * GROUPS

    def body(list_ref, place_ref, *refs):
        own_keys, own_values, *others = refs[: len(sources)]
        keys_out, values_out = refs[len(sources) :]
        here = place_ref[1] * GROUPS + place_ref[0]
        number = list_ref[0]

        def rows(i):
            return pl.ds(pl.multiple_of(i * PAGE, PAGE), PAGE)

        def collect(i, carry):
            slot = list_ref[1 + i]
            device = slot // pages
            page = slot - device * pages
            kind = jnp.bitwise_xor(device, here)

            @pl.when(kind == 0)
            def _():
                column = pl.ds(pl.multiple_of(place_ref[1] * HD, HD), HD)
                keys_out[rows(i), :] = own_keys[page, :, column]
                values_out[rows(i), :] = own_values[page, :, column]

            for which, other in enumerate(others):

                @pl.when(kind == which + 1)
                def _():
                    keys_out[rows(i), :] = other[0, page]
                    values_out[rows(i), :] = other[1, page]

            return carry

        lax.fori_loop(0, number, collect, 0)

        def clear(i, carry):
            values_out[rows(i), :] = jnp.zeros((PAGE, HD), BF16)
            return carry

        lax.fori_loop(number, jnp.minimum(number + CHUNK - 1, slots), clear, 0)

    return pl.pallas_call(
        body,
        in_specs=[SMEM, SMEM] + [VMEM] * len(sources),
        out_specs=[VMEM, VMEM],
        out_shape=[
            jax.ShapeDtypeStruct((slots * PAGE, HD), BF16),
            jax.ShapeDtypeStruct((slots * PAGE, HD), BF16),
        ],
        compiler_params=params(16),
        cost_estimate=TINY,
    )(listed, place, *sources)


def attend(listed, lengths, place, fars, queries, suffix, keys, values, rows_each, weight=None):
    fetched = [] if weight is None else [weight]
    tokens = queries[0].shape[0]
    splits = tokens // rows_each
    heads = queries[0].shape[1] // HD
    rows = tokens * heads
    slots = keys.shape[0] // PAGE
    wide = CHUNK * PAGE
    parts = -(-rows // HD)
    stat_rows = -(-3 * parts // 16) * 16
    blocks = len(queries)

    def body(list_ref, len_ref, place_ref, *refs):
        if fetched:
            weight_ref, rows_out, weight_sem = refs[0], refs[-8], refs[-1]
            refs = (*refs[1:-8], *refs[-7:-1])
            start = pl.multiple_of(place_ref[1] * heads * HD, heads * HD)
            copy = pltpu.make_async_copy(
                weight_ref.at[pl.ds(start, heads * HD)], rows_out, weight_sem
            )
            copy.start()
        query_refs, refs = refs[:blocks], refs[blocks:]
        suffix_refs, refs = refs[:splits], refs[splits:]
        keys_ref, values_ref, refs = refs[0], refs[1], refs[2:]
        outs, (stacked, scores, top, total, column, stats) = refs[:blocks], refs[blocks:]
        count = list_ref[0]
        turns = lax.div(count + (CHUNK - 1), CHUNK)
        group, split, z_here = place_ref[0], place_ref[1], place_ref[3]

        def places(z, axis):
            index = lax.broadcasted_iota(jnp.int32, (tokens, tokens), axis)
            result = jnp.zeros((tokens, tokens), jnp.int32)
            for sub in range(splits):
                block = z * splits + jnp.bitwise_xor(split, sub)
                result = jnp.where(
                    index >= sub * rows_each, (block - sub) * rows_each + index, result
                )
            return result

        own_kv = jnp.concatenate([ref[...].astype(F32) for ref in suffix_refs], axis=0).astype(BF16)
        own_keys = own_kv[:, :HD]
        own_values = jnp.concatenate([own_kv[:, HD:], jnp.ones((tokens, HD), BF16)], axis=1)
        key_place = places(z_here, 1)
        for b in range(blocks):
            q = jnp.concatenate(
                [query_refs[b][:, h * HD : (h + 1) * HD].astype(F32) for h in range(heads)], axis=0
            ).astype(BF16)
            stacked[b] = q
            query_place = places(jnp.bitwise_xor(z_here, fars[b]), 0)
            begins = jnp.zeros((tokens, tokens), jnp.int32)
            edge = jnp.int32(0)
            for r in range(REQS):
                edge = edge + len_ref[group, r]
                begins = jnp.where(query_place >= edge, edge, begins)
            seen = jnp.logical_and(key_place <= query_place, key_place >= begins)
            seen = jnp.concatenate([seen.astype(F32)] * heads, axis=0)
            own = lax.dot_general(q, own_keys, NT, preferred_element_type=F32)
            own = jnp.where(seen > 0.0, own, LOW)
            highest = jnp.max(own, axis=1, keepdims=True)
            weights = jnp.exp2((own - highest) * EXP2_SCALE) * seen
            total[b] = jnp.dot(weights.astype(BF16), own_values, preferred_element_type=F32)
            top[b] = jnp.broadcast_to(highest, (rows, HD))

        def score(b, c):
            span = pl.ds(pl.multiple_of(c * wide, wide), wide)
            scores[b] = lax.dot_general(
                stacked[b], keys_ref[span, :], NT, preferred_element_type=F32
            )

        def turn(c, last):
            span = pl.ds(pl.multiple_of(c * wide, wide), wide)
            chunk_values = jnp.concatenate(
                [values_ref[span, :], jnp.ones((wide, HD), BF16)], axis=1
            )
            for b in range(blocks):
                pieces = [scores[b, :, j * PAGE : (j + 1) * PAGE] for j in range(CHUNK)]
                if last:
                    pieces = [
                        jnp.where(c * CHUNK + j < count, piece, LOW)
                        for j, piece in enumerate(pieces)
                    ]
                best = functools.reduce(jnp.maximum, pieces)
                before = top[b]
                highest = jnp.maximum(before, jnp.max(best, axis=1, keepdims=True))
                weights = jnp.concatenate(
                    [jnp.exp2((piece - highest) * EXP2_SCALE).astype(BF16) for piece in pieces],
                    axis=1,
                )
                factor = jnp.exp2((before - highest) * EXP2_SCALE)
                added = jnp.dot(weights, chunk_values, preferred_element_type=F32)
                total[b] = total[b] * jnp.concatenate([factor, factor], axis=1) + added
                top[b] = highest
                if not last:
                    score(b, c + 1)

        def full_turn(c, carry):
            turn(c, False)
            return carry

        for b in range(blocks):
            score(b, 0)
        lax.fori_loop(0, turns - 1, full_turn, 0)

        @pl.when(turns > 0)
        def _():
            turn(turns - 1, True)

        for b in range(blocks):
            sums = total[b, :, HD:]
            some = sums > 0.0
            safe = jnp.where(some, sums, 1.0)
            outs[b][0:rows, :] = (total[b, :, :HD] / safe).astype(BF16)
            column[0:rows, :] = jnp.where(some, top[b] * EXP2_SCALE + jnp.log2(safe), LOW)
            stats[...] = jnp.zeros((stat_rows, HD), F32)
            for part in range(parts):
                line = column[part * HD : (part + 1) * HD, :].T[0:1, :]
                for piece in range(3):
                    rounded = line.astype(BF16).astype(F32)
                    stats[3 * part + piece : 3 * part + piece + 1, :] = rounded
                    line = line - rounded
            outs[b][rows : rows + stat_rows, :] = stats[...].astype(BF16)
        if fetched:
            copy.wait()

    return pl.pallas_call(
        body,
        in_specs=[SMEM, SMEM, SMEM] + [HBM] * len(fetched) + [VMEM] * (blocks + splits + 2),
        out_specs=[VMEM] * blocks + [ANY] * len(fetched),
        out_shape=[jax.ShapeDtypeStruct((rows + stat_rows, HD), BF16)] * blocks
        + [jax.ShapeDtypeStruct((heads * HD, array.shape[1]), BF16) for array in fetched],
        scratch_shapes=[
            pltpu.VMEM((blocks, rows, HD), BF16),
            pltpu.VMEM((blocks, rows, wide), F32),
            pltpu.VMEM((blocks, rows, HD), F32),
            pltpu.VMEM((blocks, rows, 2 * HD), F32),
            pltpu.VMEM((parts * HD, HD), F32),
            pltpu.VMEM((stat_rows, HD), F32),
        ]
        + [pltpu.SemaphoreType.DMA] * len(fetched),
        compiler_params=params(40 if fetched else 16),
        cost_estimate=pl.CostEstimate(
            flops=4 * blocks * rows * slots * PAGE * HD,
            bytes_accessed=slots * PAGE * HD * 3,
            transcendentals=blocks * rows * slots * PAGE // 2,
        ),
    )(listed, lengths, place, *fetched, *queries, *suffix, keys, values)


def project(place, partials, weight, rows_each, splits, ranks, heads):
    tokens = rows_each * splits
    rows = tokens * heads
    parts = -(-rows // HD)
    width = weight.shape[1] // ranks

    def body(place_ref, *refs):
        count = len(partials)
        partial_refs, weight_ref, outs = refs[:count], refs[count], refs[count + 1 : -2]
        merged, attended = refs[-2:]
        for part in range(parts):
            length = min(HD, rows - part * HD)
            lines = []
            for ref in partial_refs:
                stat = ref[rows:, :].astype(F32)
                lines.append(
                    stat[3 * part : 3 * part + 1]
                    + stat[3 * part + 1 : 3 * part + 2]
                    + stat[3 * part + 2 : 3 * part + 3]
                )
            best = functools.reduce(jnp.maximum, lines)
            shares = [jnp.exp2(line - best) for line in lines]
            whole = functools.reduce(jnp.add, shares)
            mixed = jnp.zeros((length, HD), F32)
            for share, ref in zip(shares, partial_refs):
                factor = jnp.broadcast_to(share / whole, (HD, HD)).T[:length]
                mixed = mixed + factor * ref[part * HD : part * HD + length, :].astype(F32)
            merged[part * HD : part * HD + length, :] = mixed
        for h in range(heads):
            attended[:, h * HD : (h + 1) * HD] = merged[h * tokens : (h + 1) * tokens, :].astype(
                BF16
            )
        for rank in range(ranks):
            start = pl.multiple_of(jnp.bitwise_xor(place_ref[4], rank) * width, width)
            product = jnp.dot(
                attended[...], weight_ref[:, pl.ds(start, width)], preferred_element_type=F32
            )
            for sub in range(splits):
                out = outs[rank * splits + sub]
                out[...] = product[sub * rows_each : (sub + 1) * rows_each].astype(out.dtype)

    return pl.pallas_call(
        body,
        in_specs=[SMEM] + [VMEM] * (len(partials) + 1),
        out_specs=[VMEM] * (ranks * splits),
        out_shape=[
            jax.ShapeDtypeStruct((rows_each, width), BF16 if i else F32)
            for i in range(ranks * splits)
        ],
        scratch_shapes=[pltpu.VMEM((rows, HD), F32), pltpu.VMEM((tokens, heads * HD), BF16)],
        compiler_params=params(16),
        cost_estimate=pl.CostEstimate(
            flops=2 * tokens * weight.size, bytes_accessed=weight.size, transcendentals=0
        ),
    )(place, *partials, weight)


def local(
    hidden_in,
    kv_weight,
    queries,
    prefix_keys,
    prefix_values,
    page_table,
    suffix_lengths,
    out_weight,
):
    rows = hidden_in.shape[0]
    seq_count, ranks = lax.axis_size("seq"), lax.axis_size("tp")
    seq_rank, tp_rank = lax.axis_index("seq"), lax.axis_index("tp")
    pages = prefix_keys.shape[0]
    splits = prefix_keys.shape[2] // HD
    heads = queries.shape[1] // HD // splits
    prefix_len = pages * seq_count // GROUPS * PAGE
    blocks = seq_count // GROUPS
    depth = blocks // splits
    group = seq_rank % GROUPS
    block = seq_rank // GROUPS
    split = block % splits
    place = jnp.stack(
        [group, split, (block - split) * GROUPS * pages, block // splits, tp_rank]
    ).astype(jnp.int32)
    place = jnp.concatenate([place, page_table])

    def across(array, far=0, side=0, core=0):
        step = (far * splits + side) * GROUPS + core
        return lax.ppermute(array, "seq", [(i, i ^ step) for i in range(seq_count)])

    def columns(array, index, width):
        return lax.dynamic_slice_in_dim(array, index * width, width, 1)

    def quad(array, rank, side):
        step = side * GROUPS
        route = [
            (i * ranks + j, (i ^ step) * ranks + (j ^ rank))
            for i in range(seq_count)
            for j in range(ranks)
        ]
        return lax.ppermute(array, ("seq", "tp"), route)

    def columns(array, index, width):
        return lax.dynamic_slice_in_dim(array, index * width, width, array.ndim - 1)

    parts = [columns(queries, split, heads * HD)]
    for side in range(1, splits):
        parts.append(across(columns(queries, split ^ side, heads * HD), side=side))
    my_query = jnp.concatenate(parts, axis=0)
    far_queries = [my_query] + [across(my_query, far=far) for far in range(1, depth)]
    sent = [
        jnp.stack([columns(array, split ^ side, HD) for array in (prefix_keys, prefix_values)])
        for side in range(splits)
    ]
    arrived = [across(sent[side], side=side) for side in range(1, splits)]
    sources = [prefix_keys, prefix_values, across(sent[0], core=1)]

    *projected, listed = project_kv(
        hidden_in, kv_weight, place, ranks, pages * splits * GROUPS, my_query
    )
    others = [
        lax.ppermute(projected[rank], "tp", [(i, i ^ rank) for i in range(ranks)])
        for rank in range(1, ranks)
    ]
    late = (far_queries[-1][0, 0] * 0).astype(jnp.int32)
    lengths = jnp.sum(
        jnp.where(jnp.arange(GROUPS)[:, None] == group, suffix_lengths + late, 0), axis=0
    )
    ends = jnp.sum(
        jnp.where(jnp.arange(REQS)[None, :] <= jnp.arange(REQS)[:, None], lengths[None, :], 0),
        axis=1,
    )
    within = block * rows + jnp.arange(rows, dtype=jnp.int32)
    begins = jnp.max(jnp.where(within[:, None] >= ends[None, :], ends[None, :], 0), axis=1)
    positions = prefix_len + within - begins
    half = HD // 2
    frequency = jnp.power(500000.0, -(jnp.arange(half, dtype=F32) * 2.0 / HD))
    angles = positions.astype(F32)[:, None] * frequency[None, :]
    cosine, sine = jnp.cos(angles), jnp.sin(angles)
    cosine = jnp.concatenate([cosine, cosine], axis=1)
    sine = jnp.concatenate([-sine, sine], axis=1)
    new_pages, *suffix = finish_kv(place, projected[0], others, cosine, sine, splits)
    suffix = suffix[:1] + [across(suffix[side], side=side) for side in range(1, splits)]

    for array in arrived:
        array = array_after(array, projected[0], *far_queries[1:])
        sources += [array, across(array, core=1)]
    keys, values = collect_pages(listed, place, sources, pages, splits)

    returned = []
    order = list(range(depth - 1, -1, -1))
    calls = [order[i : i + BLOCKS] for i in range(0, depth - BLOCKS, BLOCKS)]
    calls += [[far] for far in order[len(calls) * BLOCKS :]]
    for i, fars in enumerate(calls):
        sums = attend(
            listed, suffix_lengths, place, fars, [far_queries[far] for far in fars],
            suffix, keys, values, rows, None if i else out_weight,
        )
        if not i:
            weight = sums[-1]
        returned += [across(part, far=far) if far else part for far, part in zip(fars, sums)]

    products = project(place, returned, weight, rows, splits, ranks, heads)
    hidden = products[0]
    for rank in range(ranks):
        for side in range(splits):
            if rank or side:
                hidden = hidden + quad(products[rank * splits + side], rank, side).astype(F32)
    return (hidden.astype(BF16), new_pages)


def solution(mesh):
    return jax.shard_map(
        local,
        mesh=mesh,
        in_specs=(
            P("seq", "tp"),
            P("tp", None),
            P("seq", "tp"),
            P("seq", None, "tp"),
            P("seq", None, "tp"),
            P(),
            P(),
            P("tp", None),
        ),
        out_specs=(P("seq", "tp"), P("seq", "tp")),
        check_vma=False,
    )
```
